128 devices in a mesh: freq: 8 (over y, core), space: 16 (over x, z).
Axes of the slice: x: 4, y: 4, z: 4, core: 2. Of those that a mesh axis runs over, the one named last changes fastest.
Arguments:
- traces: float32 [1024, 512, 256], P(('freq', 'space')), may hold values from -50 to 50
- probes: float32 [16, 128, 64], P('freq'), may hold values from -0.5 to 0.5
Outputs:
- denoised: float32 [1024, 512, 256], P(('freq', 'space'))
The draws below stay inside these ranges and needn't reach their ends.
All inputs are finite; a program needn't handle non-finite values.
Results may differ from the reference program's by a relative error of at most 0.000092.
Values sent between devices are 32-bit elements; how exact they have to be, the bound alone decides.
A program may use at most 128 MiB of HBM per device.

```python
import jax
import jax.numpy as jnp
from jax import lax

NT = 1024
NX = 256
NY = 512
RANK = 64
BAND_LO = 16
NF = 16
COLUMNS = 128


def draw_traces(key, part):
    subkeys = jax.random.split(key, 4)
    noise_field = jnp.clip(jax.random.normal(subkeys[0], (NT, NY, NX), jnp.float32), -6.0, 6.0)
    inline_gain = jnp.exp(jax.random.uniform(subkeys[1], (NX,), jnp.float32, jnp.log(0.5), jnp.log(2.0)))
    rising = 3.0 ** (jnp.arange(NY, dtype=jnp.float32) / max(NY - 1, 1) - 0.5)
    cross_gain = jnp.exp(jax.random.uniform(subkeys[2], (NY,), jnp.float32, jnp.log(0.5), jnp.log(2.0))) * rising
    result = noise_field * cross_gain[None, :, None] * inline_gain[None, None, :]
    params = jax.random.uniform(subkeys[3], (4, 5), jnp.float32)
    sample_times = jnp.arange(NT, dtype=jnp.float32)[:, None, None]
    inline_axis = jnp.arange(NX, dtype=jnp.float32)[None, None, :]
    cross_axis = jnp.arange(NY, dtype=jnp.float32)[None, :, None]
    for event_index in range(4):
        onset_time = params[event_index, 0] * NT
        dip_inline = (params[event_index, 1] - 0.5) * 0.5
        dip_cross = (params[event_index, 2] - 0.5) * 0.5
        amplitude = 0.5 + params[event_index, 3]
        delay_field = sample_times - onset_time - dip_inline * inline_axis - dip_cross * cross_axis
        delay_field = jnp.mod(delay_field + NT / 2.0, NT) - NT / 2.0
        ricker_arg = (jnp.pi * (0.02 + 0.02 * params[event_index, 4]) * delay_field) ** 2
        result = result + amplitude * (1.0 - 2.0 * ricker_arg) * jnp.exp(-ricker_arg)
    return result


def block_scale(stream_key, dims, cuts, smallest, high):
    loudness = 1.0
    for dim, blocks in cuts:
        draws = jax.random.uniform(jax.random.fold_in(jax.random.fold_in(stream_key, 6), dim), (blocks,), jnp.float32, smallest / len(cuts), high / len(cuts))
        loudness = loudness * jnp.repeat(jnp.exp(draws), dims[dim] // blocks).reshape((-1,) + (1,) * (len(dims) - 1 - dim))
    return loudness


def noise(key, shape, deviation, reach, shards=(), kind=jnp.bfloat16):
    array = deviation * jax.random.normal(key, shape, jnp.float32)
    if shards:
        array = array * block_scale(key, shape, shards, -0.22, 0.18)
    return jnp.clip(array, -reach, reach).astype(kind)


def setup_inputs(seed: int = 0) -> dict:
    seeds = jax.random.split(jax.random.key(seed), 3)
    traces = draw_traces(jax.random.fold_in(seeds[2], 71), 0)
    probes = noise(seeds[1], (NF, COLUMNS, RANK), COLUMNS ** -0.5, 0.5, ((0, 8),), jnp.float32)
    return {"traces": traces, "probes": probes}


HIGHEST_PRECISION = lax.Precision.HIGHEST

def wave_table(freq_ids, time_ids, period, factor):
    phase = (freq_ids[:, None] * time_ids[None, :] % period).astype(jnp.float32) * (2.0 * jnp.pi / period)
    return jnp.stack([jnp.cos(phase), -jnp.sin(phase)]) * factor

def hankel(spectrum, window, columns):
    width = spectrum.shape[-1]
    tiled = jnp.tile(spectrum, (1, 1, window + 1))[:, :, :window * (width + 1)]
    return tiled.reshape(spectrum.shape[0], spectrum.shape[1], window, width + 1)[:, :, :, :columns]

def diag_mean(blocks, width):
    halves, channels, window, columns = blocks.shape
    padded = jnp.pad(blocks, ((0, 0), (0, 0), (0, 0), (0, width + 1 - columns)))
    flat_rows = padded.reshape(halves, channels, window * (width + 1))
    flat_rows = jnp.pad(flat_rows, ((0, 0), (0, 0), (0, width - window)))
    totals = flat_rows.reshape(halves, channels, window + 1, width).sum(axis=2)
    position = jnp.arange(width, dtype=jnp.int32)
    counts = jnp.minimum(jnp.minimum(position + 1, width - position), min(window, columns))
    return totals / counts.astype(jnp.float32)

def assemble(gram_raw, cross_raw):
    half = gram_raw.shape[-1] // 2
    diagonal_part = gram_raw[..., :half, :half] + gram_raw[..., half:, half:]
    skew_part = gram_raw[..., half:, :half] - gram_raw[..., :half, half:]
    gram_matrix = jnp.concatenate([jnp.concatenate([diagonal_part, skew_part], -1), jnp.concatenate([-skew_part, diagonal_part], -1)], -2)
    real_rows = cross_raw[..., 0, :, :]
    imag_rows = cross_raw[..., 1, :, :]
    cross_terms = jnp.concatenate([real_rows[..., :half, :] + imag_rows[..., half:, :], imag_rows[..., :half, :] - real_rows[..., half:, :]], -2)
    return (gram_matrix, cross_terms)

def denoise_slice(slice_pair):
    spectrum, probe = slice_pair
    width = spectrum.shape[-1]
    window = width // 2 + 1
    columns = width // 2
    channels = spectrum.shape[1]
    hankel_rows = hankel(spectrum, window, columns).reshape(2, channels * window, columns)
    sketch_basis = jnp.einsum('qrp,pk->rqk', hankel_rows, probe, precision=HIGHEST_PRECISION).reshape(channels * window, 2 * probe.shape[1])
    gram_raw = jnp.dot(sketch_basis.T, sketch_basis, precision=HIGHEST_PRECISION)
    cross_raw = jnp.einsum('rk,qrp->qkp', sketch_basis, hankel_rows, precision=HIGHEST_PRECISION)
    gram_matrix, cross_terms = assemble(gram_raw, cross_raw)
    lower_factor = jnp.linalg.cholesky(gram_matrix)
    coeffs = jax.scipy.linalg.cho_solve((lower_factor, True), cross_terms)
    half = coeffs.shape[0] // 2
    real_part = coeffs[:half]
    imag_part = coeffs[half:]
    mixing = jnp.stack([jnp.concatenate([real_part, -imag_part], 0), jnp.concatenate([imag_part, real_part], 0)])
    rebuilt = jnp.einsum('rk,qkp->qrp', sketch_basis, mixing, precision=HIGHEST_PRECISION)
    return diag_mean(rebuilt.reshape(2, channels, window, columns), width)

def reference(traces, probes):
    freq_ids = BAND_LO + jnp.arange(NF, dtype=jnp.int32)
    time_ids = jnp.arange(NT, dtype=jnp.int32)
    forward_table = wave_table(freq_ids, time_ids, NT, NT ** (-0.5))
    spectra = jnp.einsum('qft,tyx->fqyx', forward_table, traces, precision=HIGHEST_PRECISION)
    clean = lax.map(denoise_slice, (spectra, probes))
    inverse_table = wave_table(freq_ids, time_ids, NT, (2.0 / NF) ** 0.5)
    return jnp.einsum('qft,fqyx->tyx', inverse_table, clean, precision=HIGHEST_PRECISION)
```

```python
import functools

import jax
import jax.numpy as jnp
from jax import lax
from jax.experimental import pallas as pl
from jax.experimental.pallas import tpu as pltpu
from jax.sharding import PartitionSpec as P

MESH = pl.DeviceIdType.MESH
F32 = jnp.float32
BF16 = jnp.bfloat16
NT = 1024
BAND_LO = 16
NF = 16
WIDTH = 256
COLS = 128
RANK = 64

AXES = ((0, 1, 2), (1, 2, 0), (2, 0, 1))
TILES = (3, 3, 2)
TILE_OFF = (0, 3, 6)
OFFSETS = ((2, 0), (2, 1), (1, 0), (3, 1), (3, 0), (1, 1), (0, 1))


def dot(a, b):
    return jnp.dot(a, b, preferred_element_type=F32, precision=lax.Precision.HIGHEST)


def dot_nt(a, b):
    return lax.dot_general(
        a, b, (((1,), (1,)), ((), ())), preferred_element_type=F32, precision=lax.Precision.HIGHEST
    )


def dot_tn(a, b):
    return lax.dot_general(
        a, b, (((0,), (0,)), ((), ())), preferred_element_type=F32, precision=lax.Precision.HIGHEST
    )


def iota(shape, dim):
    return lax.broadcasted_iota(jnp.int32, shape, dim)


def roll2(a, s):
    n = WIDTH
    return pltpu.roll(pltpu.roll(a, s % n, 0), s % n, 1)


def device(pos, core):
    x, y, z = pos
    return (2 * y + core, 4 * x + z)


def wave(part, pos, row_axis_is_time):
    shape = (64, 32) if row_axis_is_time else (32, 64)
    tdim, fdim = (0, 1) if row_axis_is_time else (1, 0)
    l = iota(shape, tdim)
    fq = iota(shape, fdim)
    a = AXES[part][0]
    moving = l // 16
    x, y, z = [moving if a == n else pos[n] for n in range(3)]
    t = 256 * y + 128 * ((l // 8) & 1) + 32 * x + 8 * z + (l & 7)
    k = BAND_LO + fq // 2
    phase = ((k * t) & (NT - 1)).astype(F32) * (2.0 * jnp.pi / NT)
    return jnp.where((fq & 1) == 0, jnp.cos(phase), -jnp.sin(phase))


def spread(table, rows, cols):
    up = (iota((rows, rows // 8), 0) // 8 == iota((rows, rows // 8), 1)).astype(F32)
    across = (iota((cols // 8, cols), 1) // 8 == iota((cols // 8, cols), 0)).astype(F32)
    wide = dot(up, dot(table, across))
    keep = (iota((rows, cols), 0) & 7) == (iota((rows, cols), 1) & 7)
    return jnp.where(keep, wide, 0.0)


def kernel(
    traces, probes, out,
    a0, a1, a2, fwd, inv_hi, inv_lo, b0, b1, b2, rb0, rb1, rb2, c0, c1, c2, rc0, rc1, rc2,
    own_probe, far_probe, rs_send, rs_recv, ag,
    d0, d1, d2, rd0, rd1, rd2, re0, re1, re2, g0, g1, g2,
    sa, ra, la, sb, rb, sc, rc, sp, rp, lp, srs, rrs, sag, rag, sd, rd, se, re_, sg, rg, lg,
):
    bufs_a, bufs_b, recv_b = (a0, a1, a2), (b0, b1, b2), (rb0, rb1, rb2)
    bufs_c, recv_c = (c0, c1, c2), (rc0, rc1, rc2)
    bufs_d, recv_d, recv_e, bufs_g = (d0, d1, d2), (rd0, rd1, rd2), (re0, re1, re2), (g0, g1, g2)
    f = lax.axis_index("freq")
    s = lax.axis_index("space")
    pos = (s // 4, f // 2, lax.rem(s, 4))
    core = lax.rem(f, 2)
    x, y, z = pos
    other = 1 - core

    def along(axis, step, flip=0):
        p = list(pos)
        p[axis] = lax.rem(p[axis] + step, 4)
        return device(p, lax.rem(core + flip, 2))

    def rotated(part, last):
        a, b, _ = AXES[part]
        return (pos[a], pos[b], last)

    def unrotated(part, last):
        a, b, c = AXES[part]
        p = [None] * 3
        p[a], p[b], p[c] = x, y, last
        return tuple(p)

    def is_me(p):
        return (p[0] == x) & (p[1] == y) & (p[2] == z)

    def remote(src, dst, ssem, rsem, dev):
        return pltpu.make_async_remote_copy(
            src_ref=src, dst_ref=dst, send_sem=ssem, recv_sem=rsem, device_id=dev, device_id_type=MESH
        )

    barrier = pltpu.get_barrier_semaphore()
    near = [along(axis, step, flip) for axis in range(3) for step in (1, 2, 3) for flip in (0, 1)]
    near.append(device(pos, other))
    for dev in near:
        pl.semaphore_signal(barrier, inc=1, device_id=dev, device_id_type=MESH)
    far = [fn(part, last) for part in (1, 2) for last in range(4) for fn in (rotated, unrotated)]
    for p in far:
        @pl.when(jnp.logical_not(is_me(p)))
        def _():
            pl.semaphore_signal(barrier, inc=1, device_id=device(p, core), device_id_type=MESH)

    local = []
    for part in range(3):
        a = AXES[part][0]
        me = 2 * pos[a] + core
        n = 8 * TILES[part]
        cp = pltpu.make_async_copy(
            traces.at[:, pl.ds(pl.multiple_of(64 * me + 8 * TILE_OFF[part], 8), n)],
            bufs_a[part].at[me], la.at[part],
        )
        cp.start()
        local.append(cp)
    own_cp = pltpu.make_async_copy(probes.at[lax.rem(z, 2)], own_probe, lp)
    own_cp.start()

    peers = len(near) + len(far)
    for p in far:
        peers = peers - is_me(p).astype(jnp.int32)
    pl.semaphore_wait(barrier, peers)

    sends_a = [[None] * 7 for _ in range(3)]
    for d, (step, flip) in enumerate(OFFSETS):
        for part in range(3):
            a = AXES[part][0]
            me = 2 * pos[a] + core
            to = 2 * lax.rem(pos[a] + step, 4) + lax.rem(core + flip, 2)
            n = 8 * TILES[part]
            cp = remote(
                traces.at[:, pl.ds(pl.multiple_of(64 * to + 8 * TILE_OFF[part], 8), n)],
                bufs_a[part].at[me], sa.at[part, d], ra.at[part, d], along(a, step, flip),
            )
            cp.start()
            sends_a[part][d] = cp
    probe_cp = remote(probes.at[lax.rem(z, 2)], far_probe, sp, rp, device(pos, other))
    probe_cp.start()

    for part in range(3):
        fwd[part] = spread(wave(part, pos, False) * (NT ** -0.5), 256, 512)
    for part in range(3):
        table = spread(wave(part, pos, True) * ((2.0 / NF) ** 0.5), 512, 256)
        hi = table.astype(BF16)
        inv_hi[part] = hi
        inv_lo[part] = (table - hi.astype(F32)).astype(BF16)

    sends_b = [[None] * 3 for _ in range(3)]
    for part in range(3):
        local[part].wait()
        for cp in sends_a[part]:
            cp.wait_recv()
        for tile in range(TILES[part]):
            block = bufs_a[part][:, :, 8 * tile : 8 * tile + 8, :].reshape(512, WIDTH)
            bufs_b[part][:, tile] = dot(fwd[part], block).reshape(4, 64, WIDTH)
        b = AXES[part][1]
        for d, step in enumerate((2, 1, 3)):
            to = lax.rem(pos[b] + step, 4)
            cp = remote(bufs_b[part].at[to], recv_b[part].at[d], sb.at[part, d], rb.at[part, d], along(b, step))
            cp.start()
            sends_b[part][d] = cp

    def send_rotated(buf_at, dst_at, ssem, rsem, part, goal, slot):
        for last in range(4):
            p = goal(part, last)
            me = is_me(p)
            cp = remote(buf_at(last), dst_at(slot), ssem.at[part, last], rsem.at[part, slot], device(p, core))
            lc = pltpu.make_async_copy(buf_at(last), dst_at(slot), rsem.at[part, slot])

            @pl.when(me)
            def _():
                lc.start()

            @pl.when(jnp.logical_not(me))
            def _():
                cp.start()

    def wait_rotated_send(buf_at, dst_at, ssem, rsem, part, goal, slot):
        for last in range(4):
            p = goal(part, last)
            cp = remote(buf_at(last), dst_at(slot), ssem.at[part, last], rsem.at[part, slot], device(p, core))

            @pl.when(jnp.logical_not(is_me(p)))
            def _():
                cp.wait_send()

    def wait_rotated_recv(dst_at, rsem, part):
        for last in range(4):
            pltpu.make_async_copy(dst_at(last), dst_at(last), rsem.at[part, last]).wait()

    for part in range(3):
        for cp in sends_b[part]:
            cp.wait_recv()
        b, c = AXES[part][1:]
        total = bufs_b[part][pos[b]] + recv_b[part][0] + recv_b[part][1] + recv_b[part][2]
        for last in range(4):
            bufs_c[part][last] = total[:, 16 * last : 16 * last + 16, :]
        send_rotated(
            lambda last: bufs_c[part].at[last], lambda slot: recv_c[part].at[slot], sc, rc, part, rotated, pos[c]
        )

    spec = []
    for part in range(3):
        wait_rotated_recv(lambda slot: recv_c[part].at[slot], rc, part)
        r = recv_c[part]
        spec.append(r[0] + r[1] + r[2] + r[3])
    spec = jnp.concatenate(spec, 0).reshape(8, 2, 8, WIDTH)
    re = spec[:, 0].reshape(64, WIDTH)
    im = spec[:, 1].reshape(64, WIDTH)
    both = jnp.concatenate([re, im], 0)
    turned = jnp.concatenate([im, -re], 0)
    own_cp.wait()
    probe_cp.wait_recv()
    probe = jnp.where(core == z // 2, own_probe[...], far_probe[...])
    probe_left = jnp.concatenate([probe, jnp.zeros_like(probe)], 1)
    probe_right = jnp.concatenate([jnp.zeros_like(probe), probe], 1)

    def window_sum(m):
        acc = m
        for step in (1, 2, 4, 8, 16, 32, 64):
            acc = acc + roll2(acc, WIDTH - step)
        return acc[:COLS, :COLS] + m[COLS:, COLS:]

    cov = jnp.concatenate([window_sum(dot_tn(both, both)), window_sum(dot_tn(both, turned))], 1)
    rs_send[...] = dot_tn(probe, cov).reshape(8, 8, 2 * COLS)

    me = 2 * x + core
    sends = []
    for d, (step, flip) in enumerate(OFFSETS):
        to = 2 * lax.rem(x + step, 4) + lax.rem(core + flip, 2)
        cp = remote(rs_send.at[to], rs_recv.at[d], srs.at[d], rrs.at[d], along(0, step, flip))
        cp.start()
        sends.append(cp)
    acc = rs_send[me]
    for d, cp in enumerate(sends):
        cp.wait_recv()
        acc = acc + rs_recv[d]
    ag[me] = acc
    gathers = []
    for d, (step, flip) in enumerate(OFFSETS):
        cp = remote(ag.at[me], ag.at[me], sag.at[d], rag.at[d], along(0, step, flip))
        cp.start()
        gathers.append(cp)
    for cp in gathers:
        cp.wait_recv()
    cross = ag[...].reshape(RANK, 2 * COLS)

    gram = dot(jnp.concatenate([cross[:, :COLS], cross[:, COLS:]], 0), probe_left)
    lane = iota((RANK, COLS), 1)
    row = iota((RANK, COLS), 0)
    ident = (lane == row + RANK).astype(F32)
    ar = gram[:RANK] + ident
    ai = gram[RANK:]
    tr = [ar[8 * n : 8 * n + 8] for n in range(8)]
    ti = [ai[8 * n : 8 * n + 8] for n in range(8)]
    below = iota((8, 1), 0)
    for k in range(RANK):
        t0, r0 = divmod(k, 8)
        row_r = tr[t0][r0 : r0 + 1, :]
        row_i = ti[t0][r0 : r0 + 1, :]
        scale = 1.0 / row_r[:, k : k + 1]
        row_r = row_r * scale
        row_i = row_i * scale
        for n in range(t0, 8):
            if n == t0 and r0 == 7:
                continue
            col_r = tr[n][:, k : k + 1]
            col_i = ti[n][:, k : k + 1]
            if n == t0:
                col_r = jnp.where(below > r0, col_r, 0.0)
                col_i = jnp.where(below > r0, col_i, 0.0)
            tr[n] = tr[n] - (col_r * row_r - col_i * row_i)
            ti[n] = ti[n] - (col_r * row_i + col_i * row_r)
    ar = jnp.concatenate(tr, 0)
    ai = jnp.concatenate(ti, 0)
    diag = jnp.sum(jnp.where(lane == row, ar, 0.0), axis=1, keepdims=True)
    scale = 1.0 / diag
    lhs = jnp.where(lane < RANK, pltpu.roll(ar, RANK, 1), ai) * scale
    swapped = jnp.concatenate([-cross[:, COLS:], cross[:, :COLS]], 1)
    fx = dot(lhs, jnp.concatenate([cross, swapped], 0))
    fx_turned = jnp.concatenate([fx[:, COLS:], -fx[:, :COLS]], 1)
    pe = dot_nt(probe_right, jnp.concatenate([ar, ai], 0))
    mix = dot(pe, jnp.concatenate([fx, fx_turned], 0))

    counts = iota((1, WIDTH), 1)
    counts = jnp.minimum(jnp.minimum(counts + 1, WIDTH - counts), COLS).astype(F32)
    share = 1.0 / counts

    def smear(m):
        m = jnp.concatenate([m, jnp.zeros_like(m)], 1)
        m = jnp.concatenate([m, jnp.zeros_like(m)], 0)
        acc = m
        for step in (1, 2, 4, 8, 16, 32, 64):
            acc = acc + roll2(acc, step)
        return (acc + roll2(m, COLS)) * share

    wr = smear(mix[:, :COLS])
    wi = smear(mix[:, COLS:])
    clean_re = dot(both, wr)
    clean_im = dot(both, wi)
    cre = (clean_re[:64] - clean_im[64:]).reshape(8, 1, 8, WIDTH)
    cim = (clean_re[64:] + clean_im[:64]).reshape(8, 1, 8, WIDTH)
    clean = jnp.concatenate([cre, cim], 1).reshape(8, 16, WIDTH)

    for part in range(3):
        bufs_d[part][...] = clean[TILE_OFF[part] : TILE_OFF[part] + TILES[part]]
        send_rotated(
            lambda last: bufs_d[part], lambda slot: recv_d[part].at[slot], sd, rd, part, unrotated, z
        )
    sends_e = [[None] * 3 for _ in range(3)]
    for part in range(3):
        wait_rotated_recv(lambda slot: recv_d[part].at[slot], rd, part)
        b = AXES[part][1]
        for d, step in enumerate((2, 1, 3)):
            cp = remote(recv_d[part], recv_e[part].at[pos[b]], se.at[part, d], re_.at[part, d], along(b, step))
            cp.start()
            sends_e[part][d] = cp
        recv_e[part][pos[b]] = recv_d[part][...]

    sends_g = [[None] * 7 for _ in range(3)]
    last_local = []
    for part in range(3):
        for cp in sends_e[part]:
            cp.wait_recv()
        for tile in range(TILES[part]):
            block = recv_e[part][:, :, tile].reshape(256, WIDTH)
            hi = block.astype(BF16)
            lo = (block - hi.astype(F32)).astype(BF16)
            th, tl = inv_hi[part], inv_lo[part]
            vol = jnp.dot(th, hi, preferred_element_type=F32)
            vol = vol + jnp.dot(th, lo, preferred_element_type=F32)
            vol = vol + jnp.dot(tl, hi, preferred_element_type=F32)
            bufs_g[part][:, :, 8 * tile : 8 * tile + 8, :] = vol.reshape(8, 8, 8, WIDTH)
        a = AXES[part][0]
        me = 2 * pos[a] + core
        n = 8 * TILES[part]
        here = pl.ds(pl.multiple_of(64 * me + 8 * TILE_OFF[part], 8), n)
        for d, (step, flip) in enumerate(OFFSETS):
            to = 2 * lax.rem(pos[a] + step, 4) + lax.rem(core + flip, 2)
            cp = remote(bufs_g[part].at[to], out.at[:, here], sg.at[part, d], rg.at[part, d], along(a, step, flip))
            cp.start()
            sends_g[part][d] = cp
        cp = pltpu.make_async_copy(bufs_g[part].at[me], out.at[:, here], lg.at[part])
        cp.start()
        last_local.append(cp)

    for part in range(3):
        for cp in sends_a[part]:
            cp.wait_send()
        for cp in sends_b[part]:
            cp.wait_send()
        c = AXES[part][2]
        wait_rotated_send(
            lambda last: bufs_c[part].at[last], lambda slot: recv_c[part].at[slot], sc, rc, part, rotated, pos[c]
        )
        wait_rotated_send(
            lambda last: bufs_d[part], lambda slot: recv_d[part].at[slot], sd, rd, part, unrotated, z
        )
        for cp in sends_e[part]:
            cp.wait_send()
    probe_cp.wait_send()
    for cp in sends + gathers:
        cp.wait_send()
    for part in range(3):
        last_local[part].wait()
        for cp in sends_g[part]:
            cp.wait()


def body(traces, probes):
    def vm(*shape, dtype=F32):
        return pltpu.VMEM(shape, dtype)

    def each(make):
        return [make(n) for n in TILES]

    dma = pltpu.SemaphoreType.DMA
    scratch = (
        each(lambda n: vm(8, 8, 8 * n, WIDTH))
        + [vm(3, 256, 512), vm(3, 512, 256, dtype=BF16), vm(3, 512, 256, dtype=BF16)]
        + each(lambda n: vm(4, n, 64, WIDTH))
        + each(lambda n: vm(3, n, 64, WIDTH))
        + each(lambda n: vm(4, n, 16, WIDTH))
        + each(lambda n: vm(4, n, 16, WIDTH))
        + [vm(COLS, RANK), vm(COLS, RANK), vm(8, 8, 256), vm(7, 8, 256), vm(8, 8, 256)]
        + each(lambda n: vm(n, 16, WIDTH))
        + each(lambda n: vm(4, n, 16, WIDTH))
        + each(lambda n: vm(4, 4, n, 16, WIDTH))
        + each(lambda n: vm(8, 8, 8 * n, WIDTH))
        + [
            dma((3, 7)), dma((3, 7)), dma((3,)),
            dma((3, 3)), dma((3, 3)),
            dma((3, 4)), dma((3, 4)),
            dma, dma, dma,
            dma((7,)), dma((7,)), dma((7,)), dma((7,)),
            dma((3, 4)), dma((3, 4)),
            dma((3, 3)), dma((3, 3)),
            dma((3, 7)), dma((3, 7)), dma((3,)),
        ]
    )
    return pl.pallas_call(
        kernel,
        out_shape=jax.ShapeDtypeStruct(traces.shape, F32),
        in_specs=[pl.BlockSpec(memory_space=pl.ANY)] * 2,
        out_specs=pl.BlockSpec(memory_space=pl.ANY),
        scratch_shapes=scratch,
        compiler_params=pltpu.CompilerParams(
            collective_id=0, has_side_effects=True, vmem_limit_bytes=56 << 20
        ),
    )(traces, probes)


def solution(mesh):
    in_specs = (P(("freq", "space"), None, None), P("freq", None, None))
    out_specs = P(("freq", "space"), None, None)
    return jax.shard_map(body, mesh=mesh, in_specs=in_specs, out_specs=out_specs, check_vma=False)
```

```python
import functools

import jax
import jax.numpy as jnp
from jax import lax
from jax.experimental import pallas as pl
from jax.experimental.pallas import tpu as pltpu
from jax.sharding import PartitionSpec as P

MESH = pl.DeviceIdType.MESH
F32 = jnp.float32
BF16 = jnp.bfloat16
NT = 1024
BAND_LO = 16
NF = 16
WIDTH = 256
COLS = 128
RANK = 64

AXES = ((0, 1, 2), (1, 2, 0), (2, 0, 1))
ORDER = ((0, 0), (1, 3), (2, 6), (0, 1), (1, 4), (2, 7), (0, 2), (1, 5))
BATCHES = (ORDER[:3], ORDER[3:6], ORDER[6:])
VMEM_LIMIT = 32
OFFSETS = ((2, 0), (2, 1), (1, 0), (3, 1), (3, 0), (1, 1), (0, 1))


def dot(a, b):
    return jnp.dot(a, b, preferred_element_type=F32, precision=lax.Precision.HIGHEST)


def dot_nt(a, b):
    return lax.dot_general(
        a, b, (((1,), (1,)), ((), ())), preferred_element_type=F32, precision=lax.Precision.HIGHEST
    )


def dot_tn(a, b):
    return lax.dot_general(
        a, b, (((0,), (0,)), ((), ())), preferred_element_type=F32, precision=lax.Precision.HIGHEST
    )


def iota(shape, dim):
    return lax.broadcasted_iota(jnp.int32, shape, dim)


def roll2(a, s):
    n = WIDTH
    return pltpu.roll(pltpu.roll(a, s % n, 0), s % n, 1)


def device(pos, core):
    x, y, z = pos
    return (2 * y + core, 4 * x + z)


def wave(part, pos, row_axis_is_time):
    shape = (64, 32) if row_axis_is_time else (32, 64)
    tdim, fdim = (0, 1) if row_axis_is_time else (1, 0)
    l = iota(shape, tdim)
    fq = iota(shape, fdim)
    a = AXES[part][0]
    moving = l // 16
    x, y, z = [moving if a == n else pos[n] for n in range(3)]
    t = 256 * y + 128 * ((l // 8) & 1) + 32 * x + 8 * z + (l & 7)
    m = fq // 2
    if part == 1:
        m = 4 * (m & 3) + m // 4
    k = BAND_LO + m
    phase = ((k * t) & (NT - 1)).astype(F32) * (2.0 * jnp.pi / NT)
    return jnp.where((fq & 1) == 0, jnp.cos(phase), -jnp.sin(phase))


def spread(table, rows, cols):
    up = (iota((rows, rows // 8), 0) // 8 == iota((rows, rows // 8), 1)).astype(F32)
    across = (iota((cols // 8, cols), 1) // 8 == iota((cols // 8, cols), 0)).astype(F32)
    wide = dot(up, dot(table, across))
    keep = (iota((rows, cols), 0) & 7) == (iota((rows, cols), 1) & 7)
    return jnp.where(keep, wide, 0.0)


def kernel(
    traces, probes, out,
    buf_a, fwd, inv_hi, inv_lo, buf_b, recv_b, buf_c, recv_c,
    own_probe, far_probe, rs_send, rs_recv, ag,
    buf_d, recv_d, recv_e, buf_g,
    sa, ra, la, sb, rb, sc, rc, sp, rp, lp, srs, rrs, sag, rag, sd, rd, se, re_, sg, rg, lg,
):
    f = lax.axis_index("freq")
    s = lax.axis_index("space")
    pos = (s // 4, f // 2, lax.rem(s, 4))
    core = lax.rem(f, 2)
    x, y, z = pos
    other = 1 - core
    home = [2 * pos[AXES[part][0]] + core for part in range(3)]

    def along(axis, step, flip=0):
        p = list(pos)
        p[axis] = lax.rem(p[axis] + step, 4)
        return device(p, lax.rem(core + flip, 2))

    def owner(part, last):
        a, b = pos[AXES[part][0]], pos[AXES[part][1]]
        if part == 0:
            return (a, b, last)
        turned = lax.rem(a + last, 4)
        return (turned, last, b) if part == 1 else (turned, b, last)

    index = (z, y, z)

    def member(part, last):
        a, b, c = AXES[part]
        p = [None] * 3
        p[a] = x if part == 0 else lax.rem(x + 4 - index[part], 4)
        p[b] = z if part == 1 else y
        p[c] = last
        return tuple(p)

    def is_me(p):
        return (p[0] == x) & (p[1] == y) & (p[2] == z)

    def remote(src, dst, ssem, rsem, dev):
        return pltpu.make_async_remote_copy(
            src_ref=src, dst_ref=dst, send_sem=ssem, recv_sem=rsem, device_id=dev, device_id_type=MESH
        )

    finish = []

    def begin(cp):
        cp.start()
        finish.append(cp.wait_send)
        return cp

    def to_four(buf_at, dst, ssem, rsem, goal):
        for last in range(4):
            p = goal(last)
            me = is_me(p)
            cp = remote(buf_at(last), dst, ssem.at[last], rsem, device(p, core))
            lc = pltpu.make_async_copy(buf_at(last), dst, rsem)

            @pl.when(me)
            def _():
                lc.start()

            @pl.when(jnp.logical_not(me))
            def _():
                cp.start()

            def wait(me=me, cp=cp):
                @pl.when(jnp.logical_not(me))
                def _():
                    cp.wait_send()

            finish.append(wait)

    def from_four(buf, rsem):
        for last in range(4):
            pltpu.make_async_copy(buf.at[last], buf.at[last], rsem.at[last]).wait()

    barrier = pltpu.get_barrier_semaphore()
    near = [along(axis, step, flip) for step in (2, 1, 3) for axis in range(3) for flip in (0, 1)]
    near.append(device(pos, other))
    for dev in near:
        pl.semaphore_signal(barrier, inc=1, device_id=dev, device_id_type=MESH)

    def channels(block, tile):
        return pl.ds(pl.multiple_of(64 * block + 8 * tile, 8), 8)

    local = {}
    for part, tile in ORDER:
        me = home[part]
        cp = pltpu.make_async_copy(traces.at[:, channels(me, tile)], buf_a.at[tile, me], la.at[tile])
        cp.start()
        local[tile] = cp
    own_cp = pltpu.make_async_copy(probes.at[lax.rem(z, 2)], own_probe, lp)
    own_cp.start()
    pl.semaphore_wait(barrier, len(near))

    sends_a = {tile: [] for _, tile in ORDER}
    for batch in BATCHES:
        for d, (step, flip) in enumerate(OFFSETS):
            for part, tile in batch:
                a = AXES[part][0]
                to = 2 * lax.rem(pos[a] + step, 4) + lax.rem(core + flip, 2)
                sends_a[tile].append(begin(remote(
                    traces.at[:, channels(to, tile)], buf_a.at[tile, home[part]],
                    sa.at[tile, d], ra.at[tile, d], along(a, step, flip),
                )))
    probe_cp = begin(remote(probes.at[lax.rem(z, 2)], far_probe, sp, rp, device(pos, other)))

    for part in range(3):
        fwd[part] = spread(wave(part, pos, False) * (NT ** -0.5), 256, 512)
    for part in range(3):
        table = spread(wave(part, pos, True) * ((2.0 / NF) ** 0.5), 512, 256)
        hi = table.astype(BF16)
        inv_hi[part] = hi
        inv_lo[part] = (table - hi.astype(F32)).astype(BF16)

    sends_b = {}
    for part, tile in ORDER:
        local[tile].wait()
        for cp in sends_a[tile]:
            cp.wait_recv()
        buf_b[tile] = dot(fwd[part], buf_a[tile].reshape(512, WIDTH)).reshape(4, 64, WIDTH)
        b = AXES[part][1]
        sends_b[tile] = [
            begin(remote(
                buf_b.at[tile, lax.rem(pos[b] + step, 4)], recv_b.at[tile, d],
                sb.at[tile, d], rb.at[tile, d], along(b, step),
            ))
            for d, step in enumerate((2, 1, 3))
        ]

    for part, tile in ORDER:
        for cp in sends_b[tile]:
            cp.wait_recv()
        b, c = AXES[part][1:]
        total = buf_b[tile, pos[b]] + recv_b[tile, 0] + recv_b[tile, 1] + recv_b[tile, 2]
        buf_c[tile] = total.reshape(4, 16, WIDTH)
        to_four(
            buf_c.at[tile].at.__getitem__, recv_c.at[tile, pos[c]], sc.at[tile], rc.at[tile, pos[c]],
            functools.partial(owner, part),
        )

    spec = []
    for tile in range(8):
        from_four(recv_c.at[tile], rc.at[tile])
    r = recv_c
    spec = (r[:, 0] + r[:, 1] + r[:, 2] + r[:, 3]).reshape(8, 2, 8, WIDTH)
    re = spec[:, 0].reshape(64, WIDTH)
    im = spec[:, 1].reshape(64, WIDTH)
    both = jnp.concatenate([re, im], 0)
    turned = jnp.concatenate([im, -re], 0)
    own_cp.wait()
    probe_cp.wait_recv()
    probe_t = jnp.where(core == z // 2, own_probe[...], far_probe[...])

    def window_sum(m):
        acc = m
        for step in (1, 2, 4, 8, 16, 32, 64):
            acc = acc + roll2(acc, WIDTH - step)
        return acc[:COLS, :COLS] + m[COLS:, COLS:]

    cov = jnp.concatenate([window_sum(dot_tn(both, both)), window_sum(dot_tn(both, turned))], 1)
    rs_send[...] = dot(probe_t, cov).reshape(8, 8, 2 * COLS)

    me = 2 * x + core
    sends = []
    for d, (step, flip) in enumerate(OFFSETS):
        to = 2 * lax.rem(x + step, 4) + lax.rem(core + flip, 2)
        sends.append(begin(remote(rs_send.at[to], rs_recv.at[d], srs.at[d], rrs.at[d], along(0, step, flip))))
    acc = rs_send[me]
    for d, cp in enumerate(sends):
        cp.wait_recv()
        acc = acc + rs_recv[d]
    ag[me] = acc
    gathers = [
        begin(remote(ag.at[me], ag.at[me], sag.at[d], rag.at[d], along(0, step, flip)))
        for d, (step, flip) in enumerate(OFFSETS)
    ]
    for cp in gathers:
        cp.wait_recv()
    cross = ag[...].reshape(RANK, 2 * COLS)

    none = jnp.zeros_like(probe_t)
    probe_top = jnp.concatenate([probe_t, none], 0)
    probe_low = jnp.concatenate([none, probe_t], 0)
    gram = dot_nt(jnp.concatenate([cross[:, :COLS], cross[:, COLS:]], 0), probe_top)
    lane = iota((RANK, COLS), 1)
    row = iota((RANK, COLS), 0)
    ident = (lane == row + RANK).astype(F32)
    ar = gram[:RANK] + ident
    ai = gram[RANK:]
    tr = [ar[8 * n : 8 * n + 8] for n in range(8)]
    ti = [ai[8 * n : 8 * n + 8] for n in range(8)]
    below = iota((8, 1), 0)
    for k in range(RANK):
        t0, r0 = divmod(k, 8)
        row_r = tr[t0][r0 : r0 + 1, :]
        row_i = ti[t0][r0 : r0 + 1, :]
        scale = 1.0 / row_r[:, k : k + 1]
        row_r = row_r * scale
        row_i = row_i * scale
        for n in range(t0, 8):
            if n == t0 and r0 == 7:
                continue
            col_r = tr[n][:, k : k + 1]
            col_i = ti[n][:, k : k + 1]
            if n == t0:
                col_r = jnp.where(below > r0, col_r, 0.0)
                col_i = jnp.where(below > r0, col_i, 0.0)
            tr[n] = tr[n] - (col_r * row_r - col_i * row_i)
            ti[n] = ti[n] - (col_r * row_i + col_i * row_r)
    ar = jnp.concatenate(tr, 0)
    ai = jnp.concatenate(ti, 0)
    diag = jnp.sum(jnp.where(lane == row, ar, 0.0), axis=1, keepdims=True)
    scale = 1.0 / diag
    lhs = jnp.where(lane < RANK, pltpu.roll(ar, RANK, 1), ai) * scale
    swapped = jnp.concatenate([-cross[:, COLS:], cross[:, :COLS]], 1)
    fx = dot(lhs, jnp.concatenate([cross, swapped], 0))
    fx_turned = jnp.concatenate([fx[:, COLS:], -fx[:, :COLS]], 1)
    pe = dot_nt(probe_low.T, jnp.concatenate([ar, ai], 0))
    mix = dot(pe, jnp.concatenate([fx, fx_turned], 0))

    counts = iota((1, WIDTH), 1)
    counts = jnp.minimum(jnp.minimum(counts + 1, WIDTH - counts), COLS).astype(F32)
    share = 1.0 / counts

    def smear(m):
        m = jnp.concatenate([m, jnp.zeros_like(m)], 1)
        m = jnp.concatenate([m, jnp.zeros_like(m)], 0)
        acc = m
        for step in (1, 2, 4, 8, 16, 32, 64):
            acc = acc + roll2(acc, step)
        return (acc + roll2(m, COLS)) * share

    wr = smear(mix[:, :COLS])
    wi = smear(mix[:, COLS:])
    clean_re = dot(both, wr)
    clean_im = dot(both, wi)
    cre = (clean_re[:64] - clean_im[64:]).reshape(8, 1, 8, WIDTH)
    cim = (clean_re[64:] + clean_im[:64]).reshape(8, 1, 8, WIDTH)
    clean = jnp.concatenate([cre, cim], 1).reshape(8, 16, WIDTH)

    for part, tile in ORDER:
        buf_d[tile] = clean[tile]
        to_four(
            lambda last: buf_d.at[tile], recv_d.at[tile, index[part]], sd.at[tile], rd.at[tile, index[part]],
            functools.partial(member, part),
        )
    sends_e = {}
    for part, tile in ORDER:
        from_four(recv_d.at[tile], rd.at[tile])
        b = AXES[part][1]
        sends_e[tile] = [
            begin(remote(recv_d.at[tile], recv_e.at[tile, pos[b]], se.at[tile, d], re_.at[tile, d], along(b, step)))
            for d, step in enumerate((2, 1, 3))
        ]
        recv_e[tile, pos[b]] = recv_d[tile]

    sends_g = []
    for part, tile in ORDER:
        for cp in sends_e[tile]:
            cp.wait_recv()
        block = recv_e[tile].reshape(256, WIDTH)
        hi = block.astype(BF16)
        lo = (block - hi.astype(F32)).astype(BF16)
        th, tl = inv_hi[part], inv_lo[part]
        vol = jnp.dot(th, hi, preferred_element_type=F32)
        vol = vol + jnp.dot(th, lo, preferred_element_type=F32)
        vol = vol + jnp.dot(tl, hi, preferred_element_type=F32)
        buf_g[tile] = vol.reshape(8, 8, 8, WIDTH)
        a = AXES[part][0]
        here = channels(home[part], tile)
        for d, (step, flip) in enumerate(OFFSETS):
            to = 2 * lax.rem(pos[a] + step, 4) + lax.rem(core + flip, 2)
            sends_g.append(begin(remote(
                buf_g.at[tile, to], out.at[:, here], sg.at[tile, d], rg.at[tile, d], along(a, step, flip)
            )))
        cp = pltpu.make_async_copy(buf_g.at[tile, home[part]], out.at[:, here], lg.at[tile])
        cp.start()
        finish.append(cp.wait)

    for cp in sends_g:
        cp.wait_recv()
    for wait in finish:
        wait()


def body(traces, probes):
    def vm(*shape, dtype=F32):
        return pltpu.VMEM(shape, dtype)

    dma = pltpu.SemaphoreType.DMA
    scratch = [
        vm(8, 8, 8, 8, WIDTH),
        vm(3, 256, 512), vm(3, 512, 256, dtype=BF16), vm(3, 512, 256, dtype=BF16),
        vm(8, 4, 64, WIDTH), vm(8, 3, 64, WIDTH),
        vm(8, 4, 16, WIDTH), vm(8, 4, 16, WIDTH),
        vm(RANK, COLS), vm(RANK, COLS), vm(8, 8, 256), vm(7, 8, 256), vm(8, 8, 256),
        vm(8, 16, WIDTH), vm(8, 4, 16, WIDTH), vm(8, 4, 4, 16, WIDTH),
        vm(8, 8, 8, 8, WIDTH),
        dma((8, 7)), dma((8, 7)), dma((8,)),
        dma((8, 3)), dma((8, 3)),
        dma((8, 4)), dma((8, 4)),
        dma, dma, dma,
        dma((7,)), dma((7,)), dma((7,)), dma((7,)),
        dma((8, 4)), dma((8, 4)),
        dma((8, 3)), dma((8, 3)),
        dma((8, 7)), dma((8, 7)), dma((8,)),
    ]
    return pl.pallas_call(
        kernel,
        out_shape=jax.ShapeDtypeStruct(traces.shape, F32),
        in_specs=[pl.BlockSpec(memory_space=pltpu.HBM), pl.BlockSpec(memory_space=pl.ANY)],
        out_specs=pl.BlockSpec(memory_space=pl.ANY),
        scratch_shapes=scratch,
        compiler_params=pltpu.CompilerParams(
            collective_id=0, has_side_effects=True, vmem_limit_bytes=VMEM_LIMIT << 20
        ),
    )(traces, jnp.swapaxes(probes, 1, 2))


def solution(mesh):
    in_specs = (P(("freq", "space"), None, None), P("freq", None, None))
    out_specs = P(("freq", "space"), None, None)
    return jax.shard_map(body, mesh=mesh, in_specs=in_specs, out_specs=out_specs, check_vma=False)
```

```python
import functools

import jax
import jax.numpy as jnp
from jax import lax
from jax.experimental import pallas as pl
from jax.experimental.pallas import tpu as pltpu
from jax.sharding import PartitionSpec as P

MESH = pl.DeviceIdType.MESH
F32 = jnp.float32
BF16 = jnp.bfloat16
NT = 1024
BAND_LO = 16
NF = 16
WIDTH = 256
COLS = 128
RANK = 64

AXES = ((0, 1, 2), (0, 2, 1), (1, 2, 0), (2, 1, 0))
KINDS = (0, 0, 1, 1, 2, 2, 3, 3)
BATCHES = ((0, 4, 6), (2, 5, 7), (1,), (3,))
ORDER = (0, 4, 6, 2, 5, 7, 1, 3)
BACK = (0, 2, 1, 3, 4, 6, 5, 7)
OFFSETS = ((2, 0), (2, 1), (1, 0), (3, 1), (3, 0), (1, 1), (0, 1))
VMEM_LIMIT = 46
OFFSETS = ((2, 0), (2, 1), (1, 0), (3, 1), (3, 0), (1, 1), (0, 1))


def dot(a, b):
    return jnp.dot(a, b, preferred_element_type=F32, precision=lax.Precision.HIGHEST)


def dot_nt(a, b):
    return lax.dot_general(
        a, b, (((1,), (1,)), ((), ())), preferred_element_type=F32, precision=lax.Precision.HIGHEST
    )


def dot_tn(a, b):
    return lax.dot_general(
        a, b, (((0,), (0,)), ((), ())), preferred_element_type=F32, precision=lax.Precision.HIGHEST
    )


def iota(shape, dim):
    return lax.broadcasted_iota(jnp.int32, shape, dim)


def roll2(a, s):
    n = WIDTH
    return pltpu.roll(pltpu.roll(a, s % n, 0), s % n, 1)


def device(pos, core):
    x, y, z = pos
    return (2 * y + core, 4 * x + z)


def wave(kind, pos, row_axis_is_time):
    shape = (64, 32) if row_axis_is_time else (32, 64)
    tdim, fdim = (0, 1) if row_axis_is_time else (1, 0)
    l = iota(shape, tdim)
    fq = iota(shape, fdim)
    a = AXES[kind][0]
    moving = l // 16
    x, y, z = [moving if a == n else pos[n] for n in range(3)]
    t = 256 * y + 128 * ((l // 8) & 1) + 32 * x + 8 * z + (l & 7)
    m = fq // 2
    if kind in (1, 2):
        m = 4 * (m & 3) + m // 4
    k = BAND_LO + m
    phase = ((k * t) & (NT - 1)).astype(F32) * (2.0 * jnp.pi / NT)
    return jnp.where((fq & 1) == 0, jnp.cos(phase), -jnp.sin(phase))


def spread(table, rows, cols):
    up = (iota((rows, rows // 8), 0) // 8 == iota((rows, rows // 8), 1)).astype(F32)
    across = (iota((cols // 8, cols), 1) // 8 == iota((cols // 8, cols), 0)).astype(F32)
    wide = dot(up, dot(table, across))
    keep = (iota((rows, cols), 0) & 7) == (iota((rows, cols), 1) & 7)
    return jnp.where(keep, wide, 0.0)


def kernel(
    traces, probes, out,
    buf_a, fwd, inv_hi, inv_lo, buf_b, recv_b, buf_c, recv_c,
    own_probe, far_probe, rs_send, rs_recv, ag,
    buf_d, recv_d, recv_e, buf_g,
    sa, ra, la, sb, rb, sc, rc, sp, rp, lp, srs, rrs, sag, rag, sd, rd, se, re_, sg, rg, lg,
):
    f = lax.axis_index("freq")
    s = lax.axis_index("space")
    pos = (s // 4, f // 2, lax.rem(s, 4))
    core = lax.rem(f, 2)
    x, y, z = pos
    other = 1 - core
    home = [2 * pos[AXES[kind][0]] + core for kind in range(4)]

    def along(axis, step, flip=0):
        p = list(pos)
        p[axis] = lax.rem(p[axis] + step, 4)
        return device(p, lax.rem(core + flip, 2))

    def owner(kind, last):
        a, b = pos[AXES[kind][0]], pos[AXES[kind][1]]
        if kind > 1:
            a = lax.rem(a + last, 4)
        return (a, last, b) if kind in (1, 2) else (a, b, last)

    index = (z, y, y, z)

    def member(kind, last):
        a, b, c = AXES[kind]
        p = [None] * 3
        p[a] = x if kind < 2 else lax.rem(x + 4 - index[kind], 4)
        p[b] = z if kind in (1, 2) else y
        p[c] = last
        return tuple(p)

    def is_me(p):
        return (p[0] == x) & (p[1] == y) & (p[2] == z)

    def remote(src, dst, ssem, rsem, dev):
        return pltpu.make_async_remote_copy(
            src_ref=src, dst_ref=dst, send_sem=ssem, recv_sem=rsem, device_id=dev, device_id_type=MESH
        )

    finish = []

    def begin(cp):
        cp.start()
        finish.append(cp.wait_send)
        return cp

    def to_four(buf_at, dst, ssem, rsem, goal):
        for last in range(4):
            p = goal(last)
            me = is_me(p)
            cp = remote(buf_at(last), dst, ssem.at[last], rsem, device(p, core))
            lc = pltpu.make_async_copy(buf_at(last), dst, rsem)

            @pl.when(me)
            def _():
                lc.start()

            @pl.when(jnp.logical_not(me))
            def _():
                cp.start()

            def wait(me=me, cp=cp):
                @pl.when(jnp.logical_not(me))
                def _():
                    cp.wait_send()

            finish.append(wait)

    def from_four(buf, rsem):
        for last in range(4):
            pltpu.make_async_copy(buf.at[last], buf.at[last], rsem.at[last]).wait()

    barrier = pltpu.get_barrier_semaphore()
    near = [along(axis, step, flip) for step in (2, 1, 3) for axis in range(3) for flip in (0, 1)]
    near.append(device(pos, other))
    for dev in near:
        pl.semaphore_signal(barrier, inc=1, device_id=dev, device_id_type=MESH)

    def channels(block, tile):
        return pl.ds(pl.multiple_of(64 * block + 8 * tile, 8), 8)

    local = {}
    for tile in ORDER:
        me = home[KINDS[tile]]
        cp = pltpu.make_async_copy(traces.at[:, channels(me, tile)], buf_a.at[tile, me], la.at[tile])
        cp.start()
        local[tile] = cp
    own_cp = pltpu.make_async_copy(probes.at[lax.rem(z, 2)], own_probe, lp)
    own_cp.start()
    pl.semaphore_wait(barrier, len(near))

    sends_a = {tile: [] for tile in ORDER}
    for batch in BATCHES:
        for d, (step, flip) in enumerate(OFFSETS):
            for tile in batch:
                kind = KINDS[tile]
                a = AXES[kind][0]
                to = 2 * lax.rem(pos[a] + step, 4) + lax.rem(core + flip, 2)
                sends_a[tile].append(begin(remote(
                    traces.at[:, channels(to, tile)], buf_a.at[tile, home[kind]],
                    sa.at[tile, d], ra.at[tile, d], along(a, step, flip),
                )))
    probe_cp = begin(remote(probes.at[lax.rem(z, 2)], far_probe, sp, rp, device(pos, other)))

    for kind in range(4):
        fwd[kind] = spread(wave(kind, pos, False) * (NT ** -0.5), 256, 512)

    sends_b = {}

    def to_quads(tile):
        kind = KINDS[tile]
        local[tile].wait()
        for cp in sends_a[tile]:
            cp.wait_recv()
        buf_b[tile] = dot(fwd[kind], buf_a[tile].reshape(512, WIDTH)).reshape(4, 64, WIDTH)
        b = AXES[kind][1]
        sends_b[tile] = [
            begin(remote(
                buf_b.at[tile, lax.rem(pos[b] + step, 4)], recv_b.at[tile, d],
                sb.at[tile, d], rb.at[tile, d], along(b, step),
            ))
            for d, step in enumerate((2, 1, 3))
        ]

    def to_owners(tile):
        kind = KINDS[tile]
        for cp in sends_b[tile]:
            cp.wait_recv()
        b, c = AXES[kind][1:]
        total = buf_b[tile, pos[b]] + recv_b[tile, 0] + recv_b[tile, 1] + recv_b[tile, 2]
        buf_c[tile] = total.reshape(4, 16, WIDTH)
        to_four(
            buf_c.at[tile].at.__getitem__, recv_c.at[tile, pos[c]], sc.at[tile], rc.at[tile, pos[c]],
            functools.partial(owner, kind),
        )

    for n, batch in enumerate(BATCHES):
        for tile in batch:
            to_quads(tile)
        if n == 2:
            for kind in range(4):
                table = spread(wave(kind, pos, True) * ((2.0 / NF) ** 0.5), 512, 256)
                hi = table.astype(BF16)
                inv_hi[kind] = hi
                inv_lo[kind] = (table - hi.astype(F32)).astype(BF16)
        if n:
            for tile in BATCHES[n - 1]:
                to_owners(tile)
    for tile in BATCHES[-1]:
        to_owners(tile)

    spec = []
    for tile in range(8):
        from_four(recv_c.at[tile], rc.at[tile])
    r = recv_c
    spec = (r[:, 0] + r[:, 1] + r[:, 2] + r[:, 3]).reshape(8, 2, 8, WIDTH)
    re = spec[:, 0].reshape(64, WIDTH)
    im = spec[:, 1].reshape(64, WIDTH)
    both = jnp.concatenate([re, im], 0)
    turned = jnp.concatenate([im, -re], 0)
    own_cp.wait()
    probe_cp.wait_recv()
    probe_t = jnp.where(core == z // 2, own_probe[...], far_probe[...])

    def window_sum(m):
        acc = m
        for step in (1, 2, 4, 8, 16, 32, 64):
            acc = acc + roll2(acc, WIDTH - step)
        return acc[:COLS, :COLS] + m[COLS:, COLS:]

    cov = jnp.concatenate([window_sum(dot_tn(both, both)), window_sum(dot_tn(both, turned))], 1)
    rs_send[...] = dot(probe_t, cov).reshape(8, 8, 2 * COLS)

    me = 2 * x + core
    sends = []
    for d, (step, flip) in enumerate(OFFSETS):
        to = 2 * lax.rem(x + step, 4) + lax.rem(core + flip, 2)
        sends.append(begin(remote(rs_send.at[to], rs_recv.at[d], srs.at[d], rrs.at[d], along(0, step, flip))))
    acc = rs_send[me]
    for d, cp in enumerate(sends):
        cp.wait_recv()
        acc = acc + rs_recv[d]
    ag[me] = acc
    gathers = [
        begin(remote(ag.at[me], ag.at[me], sag.at[d], rag.at[d], along(0, step, flip)))
        for d, (step, flip) in enumerate(OFFSETS)
    ]
    for cp in gathers:
        cp.wait_recv()
    cross = ag[...].reshape(RANK, 2 * COLS)

    none = jnp.zeros_like(probe_t)
    probe_top = jnp.concatenate([probe_t, none], 0)
    probe_low = jnp.concatenate([none, probe_t], 0)
    gram = dot_nt(jnp.concatenate([cross[:, :COLS], cross[:, COLS:]], 0), probe_top)
    lane = iota((RANK, COLS), 1)
    row = iota((RANK, COLS), 0)
    ident = (lane == row + RANK).astype(F32)
    ar = gram[:RANK] + ident
    ai = gram[RANK:]
    tr = [ar[8 * n : 8 * n + 8] for n in range(8)]
    ti = [ai[8 * n : 8 * n + 8] for n in range(8)]
    below = iota((8, 1), 0)
    for k in range(RANK):
        t0, r0 = divmod(k, 8)
        row_r = tr[t0][r0 : r0 + 1, :]
        row_i = ti[t0][r0 : r0 + 1, :]
        scale = 1.0 / row_r[:, k : k + 1]
        row_r = row_r * scale
        row_i = row_i * scale
        for n in range(t0, 8):
            if n == t0 and r0 == 7:
                continue
            col_r = tr[n][:, k : k + 1]
            col_i = ti[n][:, k : k + 1]
            if n == t0:
                col_r = jnp.where(below > r0, col_r, 0.0)
                col_i = jnp.where(below > r0, col_i, 0.0)
            tr[n] = tr[n] - (col_r * row_r - col_i * row_i)
            ti[n] = ti[n] - (col_r * row_i + col_i * row_r)
    ar = jnp.concatenate(tr, 0)
    ai = jnp.concatenate(ti, 0)
    diag = jnp.sum(jnp.where(lane == row, ar, 0.0), axis=1, keepdims=True)
    scale = 1.0 / diag
    lhs = jnp.where(lane < RANK, pltpu.roll(ar, RANK, 1), ai) * scale
    swapped = jnp.concatenate([-cross[:, COLS:], cross[:, :COLS]], 1)
    fx = dot(lhs, jnp.concatenate([cross, swapped], 0))
    fx_turned = jnp.concatenate([fx[:, COLS:], -fx[:, :COLS]], 1)
    pe = dot_nt(probe_low.T, jnp.concatenate([ar, ai], 0))
    mix = dot(pe, jnp.concatenate([fx, fx_turned], 0))

    counts = iota((1, WIDTH), 1)
    counts = jnp.minimum(jnp.minimum(counts + 1, WIDTH - counts), COLS).astype(F32)
    share = 1.0 / counts

    def smear(m):
        m = jnp.concatenate([m, jnp.zeros_like(m)], 1)
        m = jnp.concatenate([m, jnp.zeros_like(m)], 0)
        acc = m
        for step in (1, 2, 4, 8, 16, 32, 64):
            acc = acc + roll2(acc, step)
        return (acc + roll2(m, COLS)) * share

    wr = smear(mix[:, :COLS])
    wi = smear(mix[:, COLS:])
    clean_re = dot(both, wr)
    clean_im = dot(both, wi)
    cre = (clean_re[:64] - clean_im[64:]).reshape(8, 1, 8, WIDTH)
    cim = (clean_re[64:] + clean_im[:64]).reshape(8, 1, 8, WIDTH)
    clean = jnp.concatenate([cre, cim], 1).reshape(8, 16, WIDTH)

    for tile in BACK:
        kind = KINDS[tile]
        buf_d[tile] = clean[tile]
        to_four(
            lambda last: buf_d.at[tile], recv_d.at[tile, index[kind]], sd.at[tile], rd.at[tile, index[kind]],
            functools.partial(member, kind),
        )
    sends_e = {}
    for tile in BACK:
        kind = KINDS[tile]
        from_four(recv_d.at[tile], rd.at[tile])
        b = AXES[kind][1]
        sends_e[tile] = [
            begin(remote(recv_d.at[tile], recv_e.at[tile, pos[b]], se.at[tile, d], re_.at[tile, d], along(b, step)))
            for d, step in enumerate((2, 1, 3))
        ]
        recv_e[tile, pos[b]] = recv_d[tile]

    sends_g = []
    for tile in BACK:
        kind = KINDS[tile]
        for cp in sends_e[tile]:
            cp.wait_recv()
        block = recv_e[tile].reshape(256, WIDTH)
        hi = block.astype(BF16)
        lo = (block - hi.astype(F32)).astype(BF16)
        th, tl = inv_hi[kind], inv_lo[kind]
        vol = jnp.dot(th, hi, preferred_element_type=F32)
        vol = vol + jnp.dot(th, lo, preferred_element_type=F32)
        vol = vol + jnp.dot(tl, hi, preferred_element_type=F32)
        buf_g[tile] = vol.reshape(8, 8, 8, WIDTH)
        a = AXES[kind][0]
        here = channels(home[kind], tile)
        for d, (step, flip) in enumerate(OFFSETS):
            to = 2 * lax.rem(pos[a] + step, 4) + lax.rem(core + flip, 2)
            sends_g.append(begin(remote(
                buf_g.at[tile, to], out.at[:, here], sg.at[tile, d], rg.at[tile, d], along(a, step, flip)
            )))
        cp = pltpu.make_async_copy(buf_g.at[tile, home[kind]], out.at[:, here], lg.at[tile])
        cp.start()
        finish.append(cp.wait)

    for cp in sends_g:
        cp.wait_recv()
    for wait in finish:
        wait()


def body(traces, probes):
    def vm(*shape, dtype=F32):
        return pltpu.VMEM(shape, dtype)

    dma = pltpu.SemaphoreType.DMA
    scratch = [
        vm(8, 8, 8, 8, WIDTH),
        vm(4, 256, 512), vm(4, 512, 256, dtype=BF16), vm(4, 512, 256, dtype=BF16),
        vm(8, 4, 64, WIDTH), vm(8, 3, 64, WIDTH),
        vm(8, 4, 16, WIDTH), vm(8, 4, 16, WIDTH),
        vm(RANK, COLS), vm(RANK, COLS), vm(8, 8, 256), vm(7, 8, 256), vm(8, 8, 256),
        vm(8, 16, WIDTH), vm(8, 4, 16, WIDTH), vm(8, 4, 4, 16, WIDTH),
        vm(8, 8, 8, 8, WIDTH),
        dma((8, 7)), dma((8, 7)), dma((8,)),
        dma((8, 3)), dma((8, 3)),
        dma((8, 4)), dma((8, 4)),
        dma, dma, dma,
        dma((7,)), dma((7,)), dma((7,)), dma((7,)),
        dma((8, 4)), dma((8, 4)),
        dma((8, 3)), dma((8, 3)),
        dma((8, 7)), dma((8, 7)), dma((8,)),
    ]
    return pl.pallas_call(
        kernel,
        out_shape=jax.ShapeDtypeStruct(traces.shape, F32),
        in_specs=[pl.BlockSpec(memory_space=pltpu.HBM), pl.BlockSpec(memory_space=pl.ANY)],
        out_specs=pl.BlockSpec(memory_space=pl.ANY),
        scratch_shapes=scratch,
        compiler_params=pltpu.CompilerParams(
            collective_id=0, has_side_effects=True, vmem_limit_bytes=VMEM_LIMIT << 20
        ),
    )(traces, jnp.swapaxes(probes, 1, 2))


def solution(mesh):
    in_specs = (P(("freq", "space"), None, None), P("freq", None, None))
    out_specs = P(("freq", "space"), None, None)
    return jax.shard_map(body, mesh=mesh, in_specs=in_specs, out_specs=out_specs, check_vma=False)
```

```python
import functools

import jax
import jax.numpy as jnp
from jax import lax
from jax.experimental import pallas as pl
from jax.experimental.pallas import tpu as pltpu
from jax.sharding import PartitionSpec as P

MESH = pl.DeviceIdType.MESH
F32 = jnp.float32
BF16 = jnp.bfloat16
NT = 1024
BAND_LO = 16
NF = 16
WIDTH = 256
COLS = 128
RANK = 64

AXES = ((0, 1, 2), (0, 2, 1), (1, 2, 0), (2, 1, 0))
KINDS = (0, 0, 1, 1, 2, 2, 3, 3)
BATCHES = ((0, 4, 6), (2, 5, 7), (1,), (3,))
ORDER = (0, 4, 6, 2, 5, 7, 1, 3)
LAST = 3
PLANE = tuple(
    (dy, dz) for dy in (2, 1, 3, 0) for dz in (2, 1, 3, 0) if (dy, dz) != (0, 0)
)
BACK = (0, 2, 1, 3, 4, 6, 5, 7)
OFFSETS = ((2, 0), (2, 1), (1, 0), (3, 1), (3, 0), (1, 1), (0, 1))
VMEM_LIMIT = 46
OFFSETS = ((2, 0), (2, 1), (1, 0), (3, 1), (3, 0), (1, 1), (0, 1))


def dot(a, b):
    return jnp.dot(a, b, preferred_element_type=F32, precision=lax.Precision.HIGHEST)


def dot_nt(a, b):
    return lax.dot_general(
        a, b, (((1,), (1,)), ((), ())), preferred_element_type=F32, precision=lax.Precision.HIGHEST
    )


def dot_tn(a, b):
    return lax.dot_general(
        a, b, (((0,), (0,)), ((), ())), preferred_element_type=F32, precision=lax.Precision.HIGHEST
    )


def iota(shape, dim):
    return lax.broadcasted_iota(jnp.int32, shape, dim)


def roll2(a, s):
    n = WIDTH
    return pltpu.roll(pltpu.roll(a, s % n, 0), s % n, 1)


def device(pos, core):
    x, y, z = pos
    return (2 * y + core, 4 * x + z)


def wave(kind, pos, row_axis_is_time):
    shape = (64, 32) if row_axis_is_time else (32, 64)
    tdim, fdim = (0, 1) if row_axis_is_time else (1, 0)
    l = iota(shape, tdim)
    fq = iota(shape, fdim)
    a = AXES[kind][0]
    moving = l // 16
    x, y, z = [moving if a == n else pos[n] for n in range(3)]
    t = 256 * y + 128 * ((l // 8) & 1) + 32 * x + 8 * z + (l & 7)
    m = fq // 2
    if kind in (1, 2):
        m = 4 * (m & 3) + m // 4
    k = BAND_LO + m
    phase = ((k * t) & (NT - 1)).astype(F32) * (2.0 * jnp.pi / NT)
    return jnp.where((fq & 1) == 0, jnp.cos(phase), -jnp.sin(phase))


def spread(table, rows, cols):
    up = (iota((rows, rows // 8), 0) // 8 == iota((rows, rows // 8), 1)).astype(F32)
    across = (iota((cols // 8, cols), 1) // 8 == iota((cols // 8, cols), 0)).astype(F32)
    wide = dot(up, dot(table, across))
    keep = (iota((rows, cols), 0) & 7) == (iota((rows, cols), 1) & 7)
    return jnp.where(keep, wide, 0.0)


def kernel(
    traces, probes, out,
    buf_a, fwd, inv_hi, inv_lo, buf_b, recv_b, buf_c, recv_c, recv_x,
    own_probe, far_probe, rs_send, rs_recv, ag, half, fr, fi,
    buf_d, recv_d, recv_e, buf_g,
    sa, ra, la, sb, rb, sc, rc, sx, rx, sp, rp, lp, srs, rrs, sag, rag, sd, rd, se, re_, sg, rg, lg,
):
    f = lax.axis_index("freq")
    s = lax.axis_index("space")
    pos = (s // 4, f // 2, lax.rem(s, 4))
    core = lax.rem(f, 2)
    x, y, z = pos
    other = 1 - core
    home = [2 * pos[AXES[kind][0]] + core for kind in range(4)]

    def along(axis, step, flip=0):
        p = list(pos)
        p[axis] = lax.rem(p[axis] + step, 4)
        return device(p, lax.rem(core + flip, 2))

    def owner(kind, last):
        a, b = pos[AXES[kind][0]], pos[AXES[kind][1]]
        if kind > 1:
            a = lax.rem(a + last, 4)
        return (a, last, b) if kind in (1, 2) else (a, b, last)

    index = (z, y, y, z)

    def member(kind, last):
        a, b, c = AXES[kind]
        p = [None] * 3
        p[a] = x if kind < 2 else lax.rem(x + 4 - index[kind], 4)
        p[b] = z if kind in (1, 2) else y
        p[c] = last
        return tuple(p)

    def is_me(p):
        return (p[0] == x) & (p[1] == y) & (p[2] == z)

    def remote(src, dst, ssem, rsem, dev):
        return pltpu.make_async_remote_copy(
            src_ref=src, dst_ref=dst, send_sem=ssem, recv_sem=rsem, device_id=dev, device_id_type=MESH
        )

    finish = []

    def begin(cp):
        cp.start()
        finish.append(cp.wait_send)
        return cp

    def to_four(buf_at, dst, ssem, rsem, goal):
        for last in range(4):
            p = goal(last)
            me = is_me(p)
            cp = remote(buf_at(last), dst, ssem.at[last], rsem, device(p, core))
            lc = pltpu.make_async_copy(buf_at(last), dst, rsem)

            @pl.when(me)
            def _():
                lc.start()

            @pl.when(jnp.logical_not(me))
            def _():
                cp.start()

            def wait(me=me, cp=cp):
                @pl.when(jnp.logical_not(me))
                def _():
                    cp.wait_send()

            finish.append(wait)

    def from_four(buf, rsem):
        for last in range(4):
            pltpu.make_async_copy(buf.at[last], buf.at[last], rsem.at[last]).wait()

    barrier = pltpu.get_barrier_semaphore()
    near = [along(axis, step, flip) for step in (2, 1, 3) for axis in range(3) for flip in (0, 1)]
    near.append(device(pos, other))
    for dev in near:
        pl.semaphore_signal(barrier, inc=1, device_id=dev, device_id_type=MESH)

    def channels(block, tile):
        return pl.ds(pl.multiple_of(64 * block + 8 * tile, 8), 8)

    local = {}
    for tile in ORDER:
        me = home[KINDS[tile]]
        cp = pltpu.make_async_copy(traces.at[:, channels(me, tile)], buf_a.at[tile, me], la.at[tile])
        cp.start()
        local[tile] = cp
    own_cp = pltpu.make_async_copy(probes.at[lax.rem(z, 2)], own_probe, lp)
    own_cp.start()
    pl.semaphore_wait(barrier, len(near))

    sends_a = {tile: [] for tile in ORDER}
    for batch in BATCHES:
        for d, (step, flip) in enumerate(OFFSETS):
            for tile in batch:
                kind = KINDS[tile]
                a = AXES[kind][0]
                to = 2 * lax.rem(pos[a] + step, 4) + lax.rem(core + flip, 2)
                sends_a[tile].append(begin(remote(
                    traces.at[:, channels(to, tile)], buf_a.at[tile, home[kind]],
                    sa.at[tile, d], ra.at[tile, d], along(a, step, flip),
                )))
    probe_cp = begin(remote(probes.at[lax.rem(z, 2)], far_probe, sp, rp, device(pos, other)))

    for kind in range(4):
        fwd[kind] = spread(wave(kind, pos, False) * (NT ** -0.5), 256, 512)

    sends_b = {}
    direct = []

    def to_quads(tile):
        kind = KINDS[tile]
        local[tile].wait()
        for cp in sends_a[tile]:
            cp.wait_recv()
        buf_b[tile] = dot(fwd[kind], buf_a[tile].reshape(512, WIDTH)).reshape(4, 64, WIDTH)
        if tile == LAST:
            for d, (dy, dz) in enumerate(PLANE):
                ty, tz = lax.rem(y + dy, 4), lax.rem(z + dz, 4)
                rows = pl.ds(pl.multiple_of(16 * ty, 16), 16)
                direct.append(begin(remote(
                    buf_b.at[LAST, tz, rows], recv_x.at[d], sx.at[d], rx.at[d], device((x, ty, tz), core)
                )))
            return
        b = AXES[kind][1]
        sends_b[tile] = [
            begin(remote(
                buf_b.at[tile, lax.rem(pos[b] + step, 4)], recv_b.at[tile, d],
                sb.at[tile, d], rb.at[tile, d], along(b, step),
            ))
            for d, step in enumerate((2, 1, 3))
        ]

    def to_owners(tile):
        kind = KINDS[tile]
        for cp in sends_b[tile]:
            cp.wait_recv()
        b, c = AXES[kind][1:]
        total = buf_b[tile, pos[b]] + recv_b[tile, 0] + recv_b[tile, 1] + recv_b[tile, 2]
        buf_c[tile] = total.reshape(4, 16, WIDTH)
        to_four(
            buf_c.at[tile].at.__getitem__, recv_c.at[tile, pos[c]], sc.at[tile], rc.at[tile, pos[c]],
            functools.partial(owner, kind),
        )

    for n, batch in enumerate(BATCHES):
        for tile in batch:
            to_quads(tile)
        if n == 2:
            for kind in range(4):
                table = spread(wave(kind, pos, True) * ((2.0 / NF) ** 0.5), 512, 256)
                hi = table.astype(BF16)
                inv_hi[kind] = hi
                inv_lo[kind] = (table - hi.astype(F32)).astype(BF16)
        if n:
            for tile in BATCHES[n - 1]:
                to_owners(tile)

    for tile in range(8):
        if tile != LAST:
            from_four(recv_c.at[tile], rc.at[tile])
    last = buf_b[LAST, z, pl.ds(pl.multiple_of(16 * y, 16), 16), :]
    for d, cp in enumerate(direct):
        cp.wait_recv()
        last = last + recv_x[d]
    r = recv_c
    spec = jnp.concatenate(
        [
            r[:LAST, 0] + r[:LAST, 1] + r[:LAST, 2] + r[:LAST, 3],
            last[None],
            r[LAST + 1 :, 0] + r[LAST + 1 :, 1] + r[LAST + 1 :, 2] + r[LAST + 1 :, 3],
        ],
        0,
    ).reshape(8, 2, 8, WIDTH)
    re = spec[:, 0].reshape(64, WIDTH)
    im = spec[:, 1].reshape(64, WIDTH)
    both = jnp.concatenate([re, im], 0)
    turned = jnp.concatenate([im, -re], 0)
    own_cp.wait()
    probe_cp.wait_recv()
    probe_t = jnp.where(core == z // 2, own_probe[...], far_probe[...])

    def window_sum(m):
        acc = m
        for step in (1, 2, 4, 8, 16, 32, 64):
            acc = acc + roll2(acc, WIDTH - step)
        return acc[:COLS, :COLS] + m[COLS:, COLS:]

    cov = jnp.concatenate([window_sum(dot_tn(both, both)), window_sum(dot_tn(both, turned))], 1)
    rs_send[...] = dot(probe_t, cov).reshape(2, 32, 2 * COLS)

    swap = begin(remote(rs_send.at[other], rs_recv.at[3], srs.at[3], rrs.at[3], device(pos, other)))
    swap.wait_recv()
    half[...] = rs_send[core] + rs_recv[3]
    sends = [
        begin(remote(half, rs_recv.at[d], srs.at[d], rrs.at[d], along(0, step)))
        for d, step in enumerate((2, 1, 3))
    ]
    for cp in sends:
        cp.wait_recv()
    ag[core] = half[...] + rs_recv[0] + rs_recv[1] + rs_recv[2]
    gather = begin(remote(ag.at[core], ag.at[core], sag, rag, device(pos, other)))
    gather.wait_recv()
    cross = ag[...].reshape(RANK, 2 * COLS)

    none = jnp.zeros_like(probe_t)
    probe_top = jnp.concatenate([probe_t, none], 0)
    probe_low = jnp.concatenate([none, probe_t], 0)
    gram = dot_nt(jnp.concatenate([cross[:, :COLS], cross[:, COLS:]], 0), probe_top)
    lane = iota((RANK, COLS), 1)
    row = iota((RANK, COLS), 0)
    ident = (lane == row + RANK).astype(F32)
    ar = gram[:RANK] + ident
    ai = gram[RANK:]
    tr = [ar[8 * n : 8 * n + 8] for n in range(8)]
    ti = [ai[8 * n : 8 * n + 8] for n in range(8)]
    below = iota((8, 1), 0)
    for k in range(0, RANK, 2):
        t0, r0 = divmod(k, 8)
        p1r, p1i = tr[t0][r0 : r0 + 1, :], ti[t0][r0 : r0 + 1, :]
        p2r, p2i = tr[t0][r0 + 1 : r0 + 2, :], ti[t0][r0 + 1 : r0 + 2, :]
        d1 = jnp.broadcast_to(p1r[:, k : k + 1], (1, COLS))
        er = jnp.broadcast_to(p1r[:, k + 1 : k + 2], (1, COLS))
        ei = jnp.broadcast_to(p1i[:, k + 1 : k + 2], (1, COLS))
        d2 = jnp.broadcast_to(p2r[:, k + 1 : k + 2], (1, COLS))
        inv1 = 1.0 / d1
        gr, gi = er * inv1, ei * inv1
        inv2 = 1.0 / (d2 - (er * gr + ei * gi))
        u2r = (p2r - (gr * p1r + gi * p1i)) * inv2
        u2i = (p2i - (gr * p1i - gi * p1r)) * inv2
        u1r = p1r * inv1 - (gr * u2r - gi * u2i)
        u1i = p1i * inv1 - (gr * u2i + gi * u2r)
        fr[k : k + 1, :] = u1r
        fi[k : k + 1, :] = u1i
        fr[k + 1 : k + 2, :] = u2r
        fi[k + 1 : k + 2, :] = u2i
        for n in range(t0, 8):
            if n == t0 and r0 == 6:
                continue
            c1r, c1i = tr[n][:, k : k + 1], ti[n][:, k : k + 1]
            c2r, c2i = tr[n][:, k + 1 : k + 2], ti[n][:, k + 1 : k + 2]
            if n == t0:
                c1r, c1i, c2r, c2i = [jnp.where(below > r0 + 1, c, 0.0) for c in (c1r, c1i, c2r, c2i)]
            tr[n], ti[n] = (
                tr[n] - ((c1r * u1r - c1i * u1i) + (c2r * u2r - c2i * u2i)),
                ti[n] - ((c1r * u1i + c1i * u1r) + (c2r * u2i + c2i * u2r)),
            )
    ar = jnp.concatenate(tr, 0)
    ai = jnp.concatenate(ti, 0)
    lhs = jnp.where(lane < RANK, pltpu.roll(fr[...], RANK, 1), fi[...])
    swapped = jnp.concatenate([-cross[:, COLS:], cross[:, :COLS]], 1)
    fx = dot(lhs, jnp.concatenate([cross, swapped], 0))
    fx_turned = jnp.concatenate([fx[:, COLS:], -fx[:, :COLS]], 1)
    pe = dot_nt(probe_low.T, jnp.concatenate([ar, ai], 0))
    mix = dot(pe, jnp.concatenate([fx, fx_turned], 0))

    counts = iota((1, WIDTH), 1)
    counts = jnp.minimum(jnp.minimum(counts + 1, WIDTH - counts), COLS).astype(F32)
    share = 1.0 / counts

    def smear(m):
        m = jnp.concatenate([m, jnp.zeros_like(m)], 1)
        m = jnp.concatenate([m, jnp.zeros_like(m)], 0)
        acc = m
        for step in (1, 2, 4, 8, 16, 32, 64):
            acc = acc + roll2(acc, step)
        return (acc + roll2(m, COLS)) * share

    wr = smear(mix[:, :COLS])
    wi = smear(mix[:, COLS:])
    clean_re = dot(both, wr)
    clean_im = dot(both, wi)
    cre = (clean_re[:64] - clean_im[64:]).reshape(8, 1, 8, WIDTH)
    cim = (clean_re[64:] + clean_im[:64]).reshape(8, 1, 8, WIDTH)
    clean = jnp.concatenate([cre, cim], 1).reshape(8, 16, WIDTH)

    for tile in BACK:
        kind = KINDS[tile]
        buf_d[tile] = clean[tile]
        to_four(
            lambda last: buf_d.at[tile], recv_d.at[tile, index[kind]], sd.at[tile], rd.at[tile, index[kind]],
            functools.partial(member, kind),
        )
    sends_e = {}
    for tile in BACK:
        kind = KINDS[tile]
        from_four(recv_d.at[tile], rd.at[tile])
        b = AXES[kind][1]
        sends_e[tile] = [
            begin(remote(recv_d.at[tile], recv_e.at[tile, pos[b]], se.at[tile, d], re_.at[tile, d], along(b, step)))
            for d, step in enumerate((2, 1, 3))
        ]
        recv_e[tile, pos[b]] = recv_d[tile]

    sends_g = []
    for tile in BACK:
        kind = KINDS[tile]
        for cp in sends_e[tile]:
            cp.wait_recv()
        block = recv_e[tile].reshape(256, WIDTH)
        hi = block.astype(BF16)
        lo = (block - hi.astype(F32)).astype(BF16)
        th, tl = inv_hi[kind], inv_lo[kind]
        vol = jnp.dot(th, hi, preferred_element_type=F32)
        vol = vol + jnp.dot(th, lo, preferred_element_type=F32)
        vol = vol + jnp.dot(tl, hi, preferred_element_type=F32)
        buf_g[tile] = vol.reshape(8, 8, 8, WIDTH)
        a = AXES[kind][0]
        here = channels(home[kind], tile)
        for d, (step, flip) in enumerate(OFFSETS):
            to = 2 * lax.rem(pos[a] + step, 4) + lax.rem(core + flip, 2)
            sends_g.append(begin(remote(
                buf_g.at[tile, to], out.at[:, here], sg.at[tile, d], rg.at[tile, d], along(a, step, flip)
            )))
        cp = pltpu.make_async_copy(buf_g.at[tile, home[kind]], out.at[:, here], lg.at[tile])
        cp.start()
        finish.append(cp.wait)

    for cp in sends_g:
        cp.wait_recv()
    for wait in finish:
        wait()


def body(traces, probes):
    def vm(*shape, dtype=F32):
        return pltpu.VMEM(shape, dtype)

    dma = pltpu.SemaphoreType.DMA
    scratch = [
        vm(8, 8, 8, 8, WIDTH),
        vm(4, 256, 512), vm(4, 512, 256, dtype=BF16), vm(4, 512, 256, dtype=BF16),
        vm(8, 4, 64, WIDTH), vm(8, 3, 64, WIDTH),
        vm(8, 4, 16, WIDTH), vm(8, 4, 16, WIDTH), vm(15, 16, WIDTH),
        vm(RANK, COLS), vm(RANK, COLS), vm(2, 32, 256), vm(4, 32, 256), vm(2, 32, 256), vm(32, 256),
        vm(RANK, COLS), vm(RANK, COLS),
        vm(8, 16, WIDTH), vm(8, 4, 16, WIDTH), vm(8, 4, 4, 16, WIDTH),
        vm(8, 8, 8, 8, WIDTH),
        dma((8, 7)), dma((8, 7)), dma((8,)),
        dma((8, 3)), dma((8, 3)),
        dma((8, 4)), dma((8, 4)), dma((15,)), dma((15,)),
        dma, dma, dma,
        dma((4,)), dma((4,)), dma, dma,
        dma((8, 4)), dma((8, 4)),
        dma((8, 3)), dma((8, 3)),
        dma((8, 7)), dma((8, 7)), dma((8,)),
    ]
    return pl.pallas_call(
        kernel,
        out_shape=jax.ShapeDtypeStruct(traces.shape, F32),
        in_specs=[pl.BlockSpec(memory_space=pltpu.HBM), pl.BlockSpec(memory_space=pl.ANY)],
        out_specs=pl.BlockSpec(memory_space=pl.ANY),
        scratch_shapes=scratch,
        compiler_params=pltpu.CompilerParams(
            collective_id=0, has_side_effects=True, vmem_limit_bytes=VMEM_LIMIT << 20
        ),
    )(traces, jnp.swapaxes(probes, 1, 2))


def solution(mesh):
    in_specs = (P(("freq", "space"), None, None), P("freq", None, None))
    out_specs = P(("freq", "space"), None, None)
    return jax.shard_map(body, mesh=mesh, in_specs=in_specs, out_specs=out_specs, check_vma=False)
```

```python
import functools

import jax
import jax.numpy as jnp
from jax import lax
from jax.experimental import pallas as pl
from jax.experimental.pallas import tpu as pltpu
from jax.sharding import PartitionSpec as P

MESH = pl.DeviceIdType.MESH
F32 = jnp.float32
BF16 = jnp.bfloat16
NT = 1024
BAND_LO = 16
NF = 16
WIDTH = 256
COLS = 128
RANK = 64

AXES = ((0, 1, 2), (0, 2, 1), (1, 2, 0), (2, 1, 0))
KINDS = (0, 0, 1, 1, 2, 2, 3, 3)
BATCHES = ((0, 4, 6), (2, 5, 7), (1,), (3,))
ORDER = (0, 4, 6, 2, 5, 7, 1, 3)
LAST = 3
PLANE = tuple(
    (dy, dz) for dy in (2, 1, 3, 0) for dz in (2, 1, 3, 0) if (dy, dz) != (0, 0)
)
BACK = (0, 2, 4, 6, 5, 7, 1, 3)
OFFSETS = ((2, 0), (2, 1), (1, 0), (3, 1), (3, 0), (1, 1), (0, 1))
VMEM_LIMIT = 46
OFFSETS = ((2, 0), (2, 1), (1, 0), (3, 1), (3, 0), (1, 1), (0, 1))


def dot(a, b):
    return jnp.dot(a, b, preferred_element_type=F32, precision=lax.Precision.HIGHEST)


def dot_nt(a, b):
    return lax.dot_general(
        a, b, (((1,), (1,)), ((), ())), preferred_element_type=F32, precision=lax.Precision.HIGHEST
    )


def dot_tn(a, b):
    return lax.dot_general(
        a, b, (((0,), (0,)), ((), ())), preferred_element_type=F32, precision=lax.Precision.HIGHEST
    )


def iota(shape, dim):
    return lax.broadcasted_iota(jnp.int32, shape, dim)


def roll2(a, s):
    n = WIDTH
    return pltpu.roll(pltpu.roll(a, s % n, 0), s % n, 1)


def device(pos, core):
    x, y, z = pos
    return (2 * y + core, 4 * x + z)


def wave(kind, pos, row_axis_is_time):
    shape = (64, 32) if row_axis_is_time else (32, 64)
    tdim, fdim = (0, 1) if row_axis_is_time else (1, 0)
    l = iota(shape, tdim)
    fq = iota(shape, fdim)
    a = AXES[kind][0]
    moving = l // 16
    x, y, z = [moving if a == n else pos[n] for n in range(3)]
    t = 256 * y + 128 * ((l // 8) & 1) + 32 * x + 8 * z + (l & 7)
    m = fq // 2
    if kind in (1, 2):
        m = 4 * (m & 3) + m // 4
    k = BAND_LO + m
    phase = ((k * t) & (NT - 1)).astype(F32) * (2.0 * jnp.pi / NT)
    return jnp.where((fq & 1) == 0, jnp.cos(phase), -jnp.sin(phase))


def spread(table, rows, cols):
    up = (iota((rows, rows // 8), 0) // 8 == iota((rows, rows // 8), 1)).astype(F32)
    across = (iota((cols // 8, cols), 1) // 8 == iota((cols // 8, cols), 0)).astype(F32)
    wide = dot(up, dot(table, across))
    keep = (iota((rows, cols), 0) & 7) == (iota((rows, cols), 1) & 7)
    return jnp.where(keep, wide, 0.0)


def kernel(
    traces, probes, out,
    buf_a, fwd, inv_hi, inv_lo, buf_b, recv_b, buf_c, recv_c, recv_x,
    own_probe, far_probe, rs_send, rs_recv, ag, half, fr, fi,
    buf_d, recv_d, recv_e, buf_g,
    sa, ra, la, sb, rb, sc, rc, sx, rx, sp, rp, lp, srs, rrs, sag, rag, sd, rd, se, re_, sg, rg, lg,
):
    f = lax.axis_index("freq")
    s = lax.axis_index("space")
    pos = (s // 4, f // 2, lax.rem(s, 4))
    core = lax.rem(f, 2)
    x, y, z = pos
    other = 1 - core
    home = [2 * pos[AXES[kind][0]] + core for kind in range(4)]

    def along(axis, step, flip=0):
        p = list(pos)
        p[axis] = lax.rem(p[axis] + step, 4)
        return device(p, lax.rem(core + flip, 2))

    def owner(kind, last):
        a, b = pos[AXES[kind][0]], pos[AXES[kind][1]]
        if kind > 1:
            a = lax.rem(a + last, 4)
        return (a, last, b) if kind in (1, 2) else (a, b, last)

    index = (z, y, y, z)

    def member(kind, last):
        a, b, c = AXES[kind]
        p = [None] * 3
        p[a] = x if kind < 2 else lax.rem(x + 4 - index[kind], 4)
        p[b] = z if kind in (1, 2) else y
        p[c] = last
        return tuple(p)

    def is_me(p):
        return (p[0] == x) & (p[1] == y) & (p[2] == z)

    def remote(src, dst, ssem, rsem, dev):
        return pltpu.make_async_remote_copy(
            src_ref=src, dst_ref=dst, send_sem=ssem, recv_sem=rsem, device_id=dev, device_id_type=MESH
        )

    finish = []

    def begin(cp):
        cp.start()
        finish.append(cp.wait_send)
        return cp

    def to_four(buf_at, dst, ssem, rsem, goal):
        for last in range(4):
            p = goal(last)
            me = is_me(p)
            cp = remote(buf_at(last), dst, ssem.at[last], rsem, device(p, core))
            lc = pltpu.make_async_copy(buf_at(last), dst, rsem)

            @pl.when(me)
            def _():
                lc.start()

            @pl.when(jnp.logical_not(me))
            def _():
                cp.start()

            def wait(me=me, cp=cp):
                @pl.when(jnp.logical_not(me))
                def _():
                    cp.wait_send()

            finish.append(wait)

    def from_four(buf, rsem):
        for last in range(4):
            pltpu.make_async_copy(buf.at[last], buf.at[last], rsem.at[last]).wait()

    barrier = pltpu.get_barrier_semaphore()
    near = [along(axis, step, flip) for step in (2, 1, 3) for axis in range(3) for flip in (0, 1)]
    near.append(device(pos, other))
    for dev in near:
        pl.semaphore_signal(barrier, inc=1, device_id=dev, device_id_type=MESH)

    def channels(block, tile):
        return pl.ds(pl.multiple_of(64 * block + 8 * tile, 8), 8)

    local = {}
    for tile in ORDER:
        me = home[KINDS[tile]]
        cp = pltpu.make_async_copy(traces.at[:, channels(me, tile)], buf_a.at[tile, me], la.at[tile])
        cp.start()
        local[tile] = cp
    own_cp = pltpu.make_async_copy(probes.at[lax.rem(z, 2)], own_probe, lp)
    own_cp.start()
    pl.semaphore_wait(barrier, len(near))

    sends_a = {tile: [] for tile in ORDER}
    for batch in BATCHES:
        for d, (step, flip) in enumerate(OFFSETS):
            for tile in batch:
                kind = KINDS[tile]
                a = AXES[kind][0]
                to = 2 * lax.rem(pos[a] + step, 4) + lax.rem(core + flip, 2)
                sends_a[tile].append(begin(remote(
                    traces.at[:, channels(to, tile)], buf_a.at[tile, home[kind]],
                    sa.at[tile, d], ra.at[tile, d], along(a, step, flip),
                )))
    probe_cp = begin(remote(probes.at[lax.rem(z, 2)], far_probe, sp, rp, device(pos, other)))

    for kind in range(4):
        fwd[kind] = spread(wave(kind, pos, False) * (NT ** -0.5), 256, 512)

    sends_b = {}
    direct = []

    def to_quads(tile):
        kind = KINDS[tile]
        local[tile].wait()
        for cp in sends_a[tile]:
            cp.wait_recv()
        buf_b[tile] = dot(fwd[kind], buf_a[tile].reshape(512, WIDTH)).reshape(4, 64, WIDTH)
        if tile == LAST:
            for d, (dy, dz) in enumerate(PLANE):
                ty, tz = lax.rem(y + dy, 4), lax.rem(z + dz, 4)
                rows = pl.ds(pl.multiple_of(16 * ty, 16), 16)
                direct.append(begin(remote(
                    buf_b.at[LAST, tz, rows], recv_x.at[d], sx.at[d], rx.at[d], device((x, ty, tz), core)
                )))
            return
        b = AXES[kind][1]
        sends_b[tile] = [
            begin(remote(
                buf_b.at[tile, lax.rem(pos[b] + step, 4)], recv_b.at[tile, d],
                sb.at[tile, d], rb.at[tile, d], along(b, step),
            ))
            for d, step in enumerate((2, 1, 3))
        ]

    def to_owners(tile):
        kind = KINDS[tile]
        for cp in sends_b[tile]:
            cp.wait_recv()
        b, c = AXES[kind][1:]
        total = buf_b[tile, pos[b]] + recv_b[tile, 0] + recv_b[tile, 1] + recv_b[tile, 2]
        buf_c[tile] = total.reshape(4, 16, WIDTH)
        to_four(
            buf_c.at[tile].at.__getitem__, recv_c.at[tile, pos[c]], sc.at[tile], rc.at[tile, pos[c]],
            functools.partial(owner, kind),
        )

    for n, batch in enumerate(BATCHES):
        for tile in batch:
            to_quads(tile)
        if n == 2:
            for kind in range(4):
                table = spread(wave(kind, pos, True) * ((2.0 / NF) ** 0.5), 512, 256)
                hi = table.astype(BF16)
                inv_hi[kind] = hi
                inv_lo[kind] = (table - hi.astype(F32)).astype(BF16)
        if n:
            for tile in BATCHES[n - 1]:
                to_owners(tile)

    for tile in range(8):
        if tile != LAST:
            from_four(recv_c.at[tile], rc.at[tile])
    own_cp.wait()
    probe_cp.wait_recv()
    probe_t = jnp.where(core == z // 2, own_probe[...], far_probe[...])
    r = recv_c

    def turn(m):
        m = m.reshape(-1, 2, 8, WIDTH)
        return jnp.concatenate([m[:, 1:], -m[:, :1]], 1).reshape(-1, WIDTH)

    low = r[:LAST, 0] + r[:LAST, 1] + r[:LAST, 2] + r[:LAST, 3]
    high = r[LAST + 1 :, 0] + r[LAST + 1 :, 1] + r[LAST + 1 :, 2] + r[LAST + 1 :, 3]
    early = jnp.concatenate([low, high], 0).reshape(-1, WIDTH)
    part_re = dot_tn(early, early)
    part_im = dot_tn(early, turn(early))
    last = buf_b[LAST, z, pl.ds(pl.multiple_of(16 * y, 16), 16), :]
    for d, cp in enumerate(direct):
        cp.wait_recv()
        last = last + recv_x[d]
    cov_re = part_re + dot_tn(last, last)
    cov_im = part_im + dot_tn(last, turn(last))
    spec = jnp.concatenate([low, last[None], high], 0).reshape(8, 2, 8, WIDTH)
    re = spec[:, 0].reshape(64, WIDTH)
    im = spec[:, 1].reshape(64, WIDTH)
    both = jnp.concatenate([re, im], 0)

    def window_sum(m):
        acc = m
        for step in (1, 2, 4, 8, 16, 32, 64):
            acc = acc + roll2(acc, WIDTH - step)
        return acc[:COLS, :COLS] + m[COLS:, COLS:]

    cov = jnp.concatenate([window_sum(cov_re), window_sum(cov_im)], 1)
    rs_send[...] = dot(probe_t, cov).reshape(2, 32, 2 * COLS)

    swap = begin(remote(rs_send.at[other], rs_recv.at[3], srs.at[3], rrs.at[3], device(pos, other)))
    swap.wait_recv()
    half[...] = rs_send[core] + rs_recv[3]
    sends = [
        begin(remote(half, rs_recv.at[d], srs.at[d], rrs.at[d], along(0, step)))
        for d, step in enumerate((2, 1, 3))
    ]
    for cp in sends:
        cp.wait_recv()
    ag[core] = half[...] + rs_recv[0] + rs_recv[1] + rs_recv[2]
    gather = begin(remote(ag.at[core], ag.at[core], sag, rag, device(pos, other)))
    gather.wait_recv()
    cross = ag[...].reshape(RANK, 2 * COLS)

    none = jnp.zeros_like(probe_t)
    probe_top = jnp.concatenate([probe_t, none], 0)
    probe_low = jnp.concatenate([none, probe_t], 0)
    gram = dot_nt(jnp.concatenate([cross[:, :COLS], cross[:, COLS:]], 0), probe_top)
    lane = iota((RANK, COLS), 1)
    row = iota((RANK, COLS), 0)
    ident = (lane == row + RANK).astype(F32)
    ar = gram[:RANK] + ident
    ai = gram[RANK:]
    tr = [ar[8 * n : 8 * n + 8] for n in range(8)]
    ti = [ai[8 * n : 8 * n + 8] for n in range(8)]
    below = iota((8, 1), 0)
    for k in range(0, RANK, 2):
        t0, r0 = divmod(k, 8)
        p1r, p1i = tr[t0][r0 : r0 + 1, :], ti[t0][r0 : r0 + 1, :]
        p2r, p2i = tr[t0][r0 + 1 : r0 + 2, :], ti[t0][r0 + 1 : r0 + 2, :]
        d1 = jnp.broadcast_to(p1r[:, k : k + 1], (1, COLS))
        er = jnp.broadcast_to(p1r[:, k + 1 : k + 2], (1, COLS))
        ei = jnp.broadcast_to(p1i[:, k + 1 : k + 2], (1, COLS))
        d2 = jnp.broadcast_to(p2r[:, k + 1 : k + 2], (1, COLS))
        inv1 = 1.0 / d1
        gr, gi = er * inv1, ei * inv1
        inv2 = 1.0 / (d2 - (er * gr + ei * gi))
        u2r = (p2r - (gr * p1r + gi * p1i)) * inv2
        u2i = (p2i - (gr * p1i - gi * p1r)) * inv2
        u1r = p1r * inv1 - (gr * u2r - gi * u2i)
        u1i = p1i * inv1 - (gr * u2i + gi * u2r)
        fr[k : k + 1, :] = u1r
        fi[k : k + 1, :] = u1i
        fr[k + 1 : k + 2, :] = u2r
        fi[k + 1 : k + 2, :] = u2i
        for n in range(t0, 8):
            if n == t0 and r0 == 6:
                continue
            c1r, c1i = tr[n][:, k : k + 1], ti[n][:, k : k + 1]
            c2r, c2i = tr[n][:, k + 1 : k + 2], ti[n][:, k + 1 : k + 2]
            if n == t0:
                c1r, c1i, c2r, c2i = [jnp.where(below > r0 + 1, c, 0.0) for c in (c1r, c1i, c2r, c2i)]
            tr[n], ti[n] = (
                tr[n] - ((c1r * u1r - c1i * u1i) + (c2r * u2r - c2i * u2i)),
                ti[n] - ((c1r * u1i + c1i * u1r) + (c2r * u2i + c2i * u2r)),
            )
    ar = jnp.concatenate(tr, 0)
    ai = jnp.concatenate(ti, 0)
    lhs = jnp.where(lane < RANK, pltpu.roll(fr[...], RANK, 1), fi[...])
    swapped = jnp.concatenate([-cross[:, COLS:], cross[:, :COLS]], 1)
    fx = dot(lhs, jnp.concatenate([cross, swapped], 0))
    fx_turned = jnp.concatenate([fx[:, COLS:], -fx[:, :COLS]], 1)
    pe = dot_nt(probe_low.T, jnp.concatenate([ar, ai], 0))
    mix = dot(pe, jnp.concatenate([fx, fx_turned], 0))

    counts = iota((1, WIDTH), 1)
    counts = jnp.minimum(jnp.minimum(counts + 1, WIDTH - counts), COLS).astype(F32)
    share = 1.0 / counts

    def smear(m):
        m = jnp.concatenate([m, jnp.zeros_like(m)], 1)
        m = jnp.concatenate([m, jnp.zeros_like(m)], 0)
        acc = m
        for step in (1, 2, 4, 8, 16, 32, 64):
            acc = acc + roll2(acc, step)
        return (acc + roll2(m, COLS)) * share

    wr = smear(mix[:, :COLS])
    wi = smear(mix[:, COLS:])
    clean_re = dot(both, wr)
    clean_im = dot(both, wi)
    cre = (clean_re[:64] - clean_im[64:]).reshape(8, 1, 8, WIDTH)
    cim = (clean_re[64:] + clean_im[:64]).reshape(8, 1, 8, WIDTH)
    clean = jnp.concatenate([cre, cim], 1).reshape(8, 16, WIDTH)

    for tile in BACK:
        kind = KINDS[tile]
        buf_d[tile] = clean[tile]
        to_four(
            lambda last: buf_d.at[tile], recv_d.at[tile, index[kind]], sd.at[tile], rd.at[tile, index[kind]],
            functools.partial(member, kind),
        )
    sends_e = {}
    for tile in BACK:
        kind = KINDS[tile]
        from_four(recv_d.at[tile], rd.at[tile])
        b = AXES[kind][1]
        sends_e[tile] = [
            begin(remote(recv_d.at[tile], recv_e.at[tile, pos[b]], se.at[tile, d], re_.at[tile, d], along(b, step)))
            for d, step in enumerate((2, 1, 3))
        ]
        recv_e[tile, pos[b]] = recv_d[tile]

    sends_g = []
    for tile in BACK:
        kind = KINDS[tile]
        for cp in sends_e[tile]:
            cp.wait_recv()
        block = recv_e[tile].reshape(256, WIDTH)
        hi = block.astype(BF16)
        lo = (block - hi.astype(F32)).astype(BF16)
        th, tl = inv_hi[kind], inv_lo[kind]
        vol = jnp.dot(th, hi, preferred_element_type=F32)
        vol = vol + jnp.dot(th, lo, preferred_element_type=F32)
        vol = vol + jnp.dot(tl, hi, preferred_element_type=F32)
        buf_g[tile] = vol.reshape(8, 8, 8, WIDTH)
        a = AXES[kind][0]
        here = channels(home[kind], tile)
        for d, (step, flip) in enumerate(OFFSETS):
            to = 2 * lax.rem(pos[a] + step, 4) + lax.rem(core + flip, 2)
            sends_g.append(begin(remote(
                buf_g.at[tile, to], out.at[:, here], sg.at[tile, d], rg.at[tile, d], along(a, step, flip)
            )))
        cp = pltpu.make_async_copy(buf_g.at[tile, home[kind]], out.at[:, here], lg.at[tile])
        cp.start()
        finish.append(cp.wait)

    for cp in sends_g:
        cp.wait_recv()
    for wait in finish:
        wait()


def body(traces, probes):
    def vm(*shape, dtype=F32):
        return pltpu.VMEM(shape, dtype)

    dma = pltpu.SemaphoreType.DMA
    scratch = [
        vm(8, 8, 8, 8, WIDTH),
        vm(4, 256, 512), vm(4, 512, 256, dtype=BF16), vm(4, 512, 256, dtype=BF16),
        vm(8, 4, 64, WIDTH), vm(8, 3, 64, WIDTH),
        vm(8, 4, 16, WIDTH), vm(8, 4, 16, WIDTH), vm(15, 16, WIDTH),
        vm(RANK, COLS), vm(RANK, COLS), vm(2, 32, 256), vm(4, 32, 256), vm(2, 32, 256), vm(32, 256),
        vm(RANK, COLS), vm(RANK, COLS),
        vm(8, 16, WIDTH), vm(8, 4, 16, WIDTH), vm(8, 4, 4, 16, WIDTH),
        vm(8, 8, 8, 8, WIDTH),
        dma((8, 7)), dma((8, 7)), dma((8,)),
        dma((8, 3)), dma((8, 3)),
        dma((8, 4)), dma((8, 4)), dma((15,)), dma((15,)),
        dma, dma, dma,
        dma((4,)), dma((4,)), dma, dma,
        dma((8, 4)), dma((8, 4)),
        dma((8, 3)), dma((8, 3)),
        dma((8, 7)), dma((8, 7)), dma((8,)),
    ]
    return pl.pallas_call(
        kernel,
        out_shape=jax.ShapeDtypeStruct(traces.shape, F32),
        in_specs=[pl.BlockSpec(memory_space=pltpu.HBM), pl.BlockSpec(memory_space=pl.ANY)],
        out_specs=pl.BlockSpec(memory_space=pl.ANY),
        scratch_shapes=scratch,
        compiler_params=pltpu.CompilerParams(
            collective_id=0, has_side_effects=True, vmem_limit_bytes=VMEM_LIMIT << 20
        ),
    )(traces, jnp.swapaxes(probes, 1, 2))


def solution(mesh):
    in_specs = (P(("freq", "space"), None, None), P("freq", None, None))
    out_specs = P(("freq", "space"), None, None)
    return jax.shard_map(body, mesh=mesh, in_specs=in_specs, out_specs=out_specs, check_vma=False)
```
